32 devices in a mesh: rows: 4 (over x, core), neur: 8 (over z, y).
Axes of the slice: x: 2, y: 2, z: 4, core: 2. Of those that a mesh axis runs over, the one named last changes fastest.
Arguments:
- tokens: bfloat16 [512, 12288], P('neur', 'rows'), may hold values from -6 to 6
- teacher_up: bfloat16 [12288, 49152], P('rows', 'neur'), may hold values from -0.0546875 to 0.0546875
- teacher_bias: float32 [49152], P('neur'), may hold values from -3 to 3
- predictor_down: bfloat16 [12288, 1024], P('rows', 'neur'), may hold values from -0.0546875 to 0.0546875
- predictor_up: bfloat16 [1024, 49152], P(None, ('neur', 'rows')), may hold values from -0.375 to 0.375
Outputs:
- teacher_relu: bfloat16 [512, 49152], P(None, ('neur', 'rows'))
- grad_down: float32 [12288, 1024], P('rows', 'neur')
- grad_up: float32 [1024, 49152], P(None, ('neur', 'rows'))
The draws below stay inside these ranges and needn't reach their ends.
All inputs are finite; a program needn't handle non-finite values.
Results may differ from the reference program's by a relative error of at most 0.0047.
Values may be sent and summed in bfloat16 or wider, within the bound.
No kernel may reach another device: no remote copies, remote signals or barrier semaphores. Data moves between devices by JAX's collectives and lax.ppermute only.
A program may use at most 128 MiB of HBM per device.

```python
import jax
import jax.numpy as jnp

D = 12288
F = 49152
R = 1024
TOKENS = 512


def strengthened(result, rng, source, target, blocks, factor):
    def block_of(dim):
        return (jnp.arange(result.shape[dim]) // (result.shape[dim] // blocks)).reshape((-1,) + (1,) * (result.ndim - 1 - dim))

    near = jax.random.permutation(rng, blocks)[block_of(target)]
    other_side = (block_of(target) + blocks // 2) % blocks
    return jnp.where((block_of(source) == near) | (block_of(source) == other_side), factor * result, result)


def shard_levels(rng, extent, shards, least, high):
    loudness, own = 1.0, jax.random.fold_in(rng, 6)
    for dim, shards_of in shards:
        steps = jnp.exp(jax.random.uniform(jax.random.fold_in(own, dim), (shards_of,), jnp.float32, least / len(shards), high / len(shards)))
        loudness = loudness * jnp.repeat(steps, extent[dim] // shards_of).reshape([-1 if axis == dim else 1 for axis in range(len(extent))])
    return loudness


def bell_draw(rng, dims, width, limit, cuts=(), held_as=jnp.bfloat16):
    result = jax.random.normal(rng, dims, jnp.float32) * width
    if len(cuts) > 0:
        result = shard_levels(rng, dims, cuts, -0.22, 0.18) * result
    return jnp.clip(result, min=-limit, max=limit).astype(held_as)


def noise_with(rng, shape, deviation, most, shards, heavy, kind=jnp.bfloat16):
    values = deviation * jax.random.normal(rng, shape, jnp.float32)
    if shards:
        values = values * shard_levels(rng, shape, shards, -0.22, 0.18)
    return jnp.clip(strengthened(values, jax.random.fold_in(rng, 3), *heavy), -most, most).astype(kind)


def setup_inputs(seed: int = 0) -> dict:
    streams_of = jax.random.split(jax.random.key(seed), 6)
    tokens = bell_draw(streams_of[0], (TOKENS, D), 1.0, 6.0, ((0, 8), (1, 4)))
    teacher_up = bell_draw(streams_of[1], (D, F), D ** -0.5, 0.0546875, ((0, 4), (1, 8)))
    teacher_bias = bell_draw(streams_of[2], (F,), 0.5, 3.0, ((0, 8),), jnp.float32)
    predictor_down = bell_draw(streams_of[3], (D, R), D ** -0.5, 0.0546875, ((0, 4), (1, 8)))
    predictor_up = noise_with(streams_of[4], (R, F), R ** -0.5, 0.375, ((1, 32),), (1, 0, 32, 2.75))
    return {"tokens": tokens, "teacher_up": teacher_up, "teacher_bias": teacher_bias, "predictor_down": predictor_down, "predictor_up": predictor_up}


loss_weight = 0.03125


def reference(tokens, teacher_up, teacher_bias, predictor_down, predictor_up):
    preact = jnp.dot(tokens, teacher_up, preferred_element_type=jnp.float32) + teacher_bias
    teacher_relu = jnp.maximum(preact, 0.0).astype(jnp.bfloat16)
    target = jax.nn.sigmoid(preact)
    hidden = jnp.dot(tokens, predictor_down, preferred_element_type=jnp.float32).astype(jnp.bfloat16)
    logits = jnp.dot(hidden, predictor_up, preferred_element_type=jnp.float32)
    residue = (loss_weight * (jax.nn.sigmoid(logits) - target)).astype(jnp.bfloat16)
    grad_up = jnp.dot(hidden.T, residue, preferred_element_type=jnp.float32)
    back = jnp.dot(residue, predictor_up.T, preferred_element_type=jnp.float32).astype(jnp.bfloat16)
    grad_down = jnp.dot(tokens.T, back, preferred_element_type=jnp.float32)
    return teacher_relu, grad_down, grad_up
```

```python
import jax
import jax.numpy as jnp
from jax import lax
from jax.experimental import pallas as pl
from jax.experimental.pallas import tpu as pltpu
from jax.sharding import PartitionSpec as P

loss_weight = 0.03125
bf16 = jnp.bfloat16
f32 = jnp.float32


def flip(value, axis, size, distance):
    return lax.ppermute(value, axis, [(i, i ^ distance) for i in range(size)])


def block(value, index, width, axis):
    return lax.dynamic_slice_in_dim(value, index * width, width, axis)


def gather_line(own, lines, size, place):
    def pairs(moves):
        return [(a * lines + y, b * lines + y) for a, b in moves for y in range(lines)]

    edge = (place == 0) | (place == 3)
    middle = pairs([(1, 2), (2, 1)])
    outward = pairs([(1, 0), (2, 3)])
    near = flip(own, "neur", size, lines)
    across = lax.ppermute(own, "neur", middle)
    far = lax.ppermute(near, "neur", middle)
    second = jnp.where(edge, lax.ppermute(across, "neur", outward), far)
    third = jnp.where(edge, lax.ppermute(far, "neur", outward), across)
    return [own, near, second, third]


def general_body(n_rows, n_neur):
    lines = 1
    while lines * lines * 4 <= n_neur:
        lines *= 2
    places = n_neur // lines
    pairs_x = n_rows // 2

    def body(tokens, teacher_up, teacher_bias, predictor_down, predictor_up):
        row = lax.axis_index("rows")
        core, x = row % 2, row // 2
        neur = lax.axis_index("neur")
        place, line = neur // lines, neur % lines
        t = tokens.shape[0]
        half_rows = t * n_neur // 2
        width = teacher_up.shape[1] // n_rows
        rank = predictor_down.shape[1]
        ranks = predictor_up.shape[0]

        if places == 4:
            column = gather_line(tokens, lines, n_neur, place)
        else:
            column = [tokens] + [flip(tokens, "neur", n_neur, d * lines) for d in range(1, places)]
        shards = []
        for shard in column:
            shards.append(shard)
            for d in range(1, lines):
                shards.append(flip(shard, "neur", n_neur, d))
        half = n_neur // 2
        within = neur % half
        side = neur // half

        def ordered(parts):
            whole = jnp.zeros((half_rows, tokens.shape[1]), bf16)
            for s, part in enumerate(parts):
                whole = lax.dynamic_update_slice_in_dim(whole, part, (within ^ s) * t, 0)
            return whole

        near_rows = ordered(shards[:half])
        far_rows = ordered(shards[half:])

        def in_order(near, far):
            return jnp.where(side == 0, jnp.concatenate([near, far]), jnp.concatenate([far, near]))

        gathered = in_order(near_rows, far_rows)

        hidden_part = jnp.dot(gathered, predictor_down, preferred_element_type=f32)
        mine = block(hidden_part, core, half_rows, 0)
        mine = mine + flip(block(hidden_part, 1 - core, half_rows, 0), "rows", n_rows, 1)
        step = 2
        while step < n_rows:
            mine = mine + flip(mine, "rows", n_rows, step)
            step *= 2
        mine = mine.astype(bf16)
        column = [mine] + [flip(mine, "neur", n_neur, d * lines) for d in range(1, places)]
        stack = jnp.stack(column)
        stacks = [stack] + [flip(stack, "neur", n_neur, e) for e in range(1, lines)]
        blocks = [stacks[d % lines][d // lines] for d in range(n_neur)]
        hidden_half = jnp.zeros((half_rows, ranks), bf16)
        for d, part in enumerate(blocks):
            hidden_half = lax.dynamic_update_slice_in_dim(hidden_half, part, (neur ^ d) * rank, 1)
        other = flip(hidden_half, "rows", n_rows, 1)
        hidden = jnp.where(
            core == 0,
            jnp.concatenate([hidden_half, other]),
            jnp.concatenate([other, hidden_half]),
        )

        bias_cols = block(teacher_bias, row, width, 0)

        def preactivation(part):
            value = jnp.dot(part, teacher_up, preferred_element_type=f32)
            value = value.reshape(part.shape[0], pairs_x, 2, width)
            keep = lax.dynamic_index_in_dim(value, core, 2, keepdims=False)
            send = lax.dynamic_index_in_dim(value, 1 - core, 2, keepdims=False)
            chip = keep + flip(send.astype(bf16), "rows", n_rows, 1)
            total = lax.dynamic_index_in_dim(chip, x, 1, keepdims=False)
            for d in range(1, pairs_x):
                away = lax.dynamic_index_in_dim(chip, x ^ d, 1, keepdims=False)
                total = total + flip(away.astype(bf16), "rows", n_rows, 2 * d)
            return total + bias_cols[None, :]

        preact = in_order(preactivation(near_rows), preactivation(far_rows))
        teacher_relu = jnp.maximum(preact, 0.0).astype(bf16)
        target = jax.nn.sigmoid(preact)
        logits = jnp.dot(hidden, predictor_up, preferred_element_type=f32)
        residue = (loss_weight * (jax.nn.sigmoid(logits) - target)).astype(bf16)
        grad_up = jnp.einsum("tr,tf->rf", hidden, residue, preferred_element_type=f32)

        back_part = jnp.einsum("tf,rf->tr", residue, predictor_up, preferred_element_type=f32)
        total = block(back_part, core, half_rows, 0)
        total = total + flip(block(back_part, 1 - core, half_rows, 0), "rows", n_rows, 1)
        total = total.reshape(half_rows, places, lines, rank)
        kept = lax.dynamic_index_in_dim(total, line, 2, keepdims=False)
        for e in range(1, lines):
            away = lax.dynamic_index_in_dim(total, line ^ e, 2, keepdims=False)
            kept = kept + flip(away.astype(bf16), "neur", n_neur, e)
        back = lax.dynamic_index_in_dim(kept, place, 1, keepdims=False)
        for d in range(1, places):
            away = lax.dynamic_index_in_dim(kept, place ^ d, 1, keepdims=False)
            back = back + flip(away.astype(bf16), "neur", n_neur, d * lines)
        step = 2
        while step < n_rows:
            back = back + flip(back, "rows", n_rows, step)
            step *= 2
        back = back.astype(bf16)
        other = flip(back, "rows", n_rows, 1)
        back = jnp.where(
            core == 0, jnp.concatenate([back, other]), jnp.concatenate([other, back])
        )
        grad_down = jnp.einsum("td,tr->dr", gathered, back, preferred_element_type=f32)
        return (teacher_relu, grad_down, grad_up)

    return body


def spot(space=pltpu.VMEM):
    return pl.BlockSpec(memory_space=space)


def shape_of(shape, dtype):
    return jax.ShapeDtypeStruct(shape, dtype)


def call(kernel, outs, ins, spaces, scratch=(), mib=12, after=(), through=(), weight=1, aliases=None, out_spaces=None):
    outs = list(outs)
    out_spaces = list(out_spaces or [pltpu.VMEM] * len(outs))
    passed = list(through)
    n_in, n_out = len(ins), len(outs)

    def body(*refs):
        end = n_in + len(passed) + len(after)
        kernel(*refs[:n_in], *refs[end : end + n_out], *refs[end + n_out + len(passed) :])

    places = [pl.ANY] * len(through)
    outs += [shape_of(value.shape, value.dtype) for value in through]
    aliased = dict(aliases or {})
    aliased.update({n_in + k: n_out + k for k in range(len(passed))})
    results = pl.pallas_call(
        body,
        out_shape=tuple(outs),
        in_specs=[spot(space) for space in list(spaces) + places + [pl.ANY] * len(after)],
        out_specs=tuple(spot(space) for space in out_spaces + places),
        scratch_shapes=list(scratch),
        input_output_aliases=aliased,
        compiler_params=pltpu.CompilerParams(vmem_limit_bytes=mib * 2**20),
        cost_estimate=pl.CostEstimate(flops=weight * 4000000000 if weight == 1 else 10**10, bytes_accessed=1000, transcendentals=0),
    )(*ins, *through, *after)
    return results


def tile_of(width):
    for tile in (512, 384, 256, 128):
        if width % tile == 0:
            return tile
    return width


def held(value):
    return pltpu.with_memory_space_constraint(value, pltpu.VMEM)


def bias_part(row, bias, width, **order):
    def kernel(row_ref, bias_ref, cols_ref):
        cols_ref[...] = bias_ref[:, pl.ds(pl.multiple_of(row_ref[0] * width, 128), width)]

    return call(
        kernel,
        [shape_of((1, width), f32)],
        [row, bias.reshape(1, bias.shape[0])],
        [pltpu.SMEM, pltpu.VMEM],
        **order,
    )


def hold(*values, **order):
    def kernel(out_ref):
        out_ref[...] = jnp.zeros_like(out_ref)

    return call(kernel, [shape_of((8, 128), f32)], [], [], through=values, **order)


def joined(refs, cols=slice(None)):
    return jnp.concatenate([ref[:, cols] for ref in refs]) if len(refs) > 1 else refs[0][:, cols]


def partial_sums(row, parts, weight, width, blocks, dtype, gots=(), plus=(), cost=1, **order):
    rows = sum(part.shape[0] for part in parts)
    depth = weight.shape[0]
    tile = tile_of(width)
    per = width // tile
    tiles = len(blocks) * per
    slots = min(tiles, 3)
    extra = [value for pair in plus for value in pair]
    heights = [pair[0].shape[0] for pair in plus]
    ins = [row, *parts, *gots, *extra, weight]

    def kernel(*refs):
        row_ref, part_refs = refs[0], refs[1 : 1 + len(parts)]
        got_refs = refs[1 + len(parts) : 1 + len(parts) + len(gots)]
        weight_ref = refs[len(ins) - 1]
        outs, (buffer, sems) = refs[len(ins) : -2], refs[-2:]
        x, core = row_ref[0] // 2, row_ref[0] % 2

        def copy(j):
            distance, keep = blocks[j // per]
            whose = (x ^ distance) * 2 + (core if keep else 1 - core)
            from_cols = pl.ds(pl.multiple_of(whose * width + (j % per) * tile, 128), tile)
            return pltpu.make_async_copy(weight_ref.at[:, from_cols], buffer.at[j % slots], sems.at[j % slots])

        for j in range(slots):
            copy(j).start()
        first = 0
        for i, height in enumerate(heights):
            a_ref, b_ref = refs[len(ins) - 1 - len(extra) + 2 * i : len(ins) + 1 - len(extra) + 2 * i]
            outs[-1][first : first + height, :] = a_ref[...] + b_ref[...]
            first += height
        part = joined(part_refs)
        for j in range(tiles):
            copy(j).wait()
            cols = slice(j % per * tile, (j % per + 1) * tile)
            value = jnp.dot(part, buffer[j % slots], preferred_element_type=f32)
            if gots:
                value = value + got_refs[j // per][:, cols].astype(f32)
            outs[j // per][:, cols] = value.astype(dtype)
            if j + slots < tiles:
                copy(j + slots).start()

    sums = [shape_of((sum(heights), extra[0].shape[1]), f32)] if extra else []
    return call(
        kernel,
        [shape_of((rows, width), dtype) for _ in blocks] + sums,
        ins,
        [pltpu.SMEM] + [pltpu.VMEM] * (len(ins) - 2) + [pl.ANY],
        scratch=[pltpu.VMEM((slots, depth, tile), bf16), pltpu.SemaphoreType.DMA((slots,))],
        mib=24,
        weight=cost,
        **order,
    )


def add_all(dtype, *groups, **order):
    rows = [group[0].shape[0] for group in groups]

    def kernel(*refs):
        out_ref, at, first = refs[-1], 0, 0
        for group, size in zip(groups, rows):
            value = refs[at][...]
            for k in range(1, len(group)):
                value = value + refs[at + k][...]
            out_ref[first : first + size, :] = value.astype(dtype)
            at, first = at + len(group), first + size

    ins = [value for group in groups for value in group]
    out = shape_of((sum(rows), groups[0][0].shape[1]), dtype)
    return call(kernel, [out], ins, [pltpu.VMEM] * len(ins), **order)


def stacked(values, **order):
    def kernel(*refs):
        for k, ref in enumerate(refs[:-1]):
            refs[-1][k] = ref[...]

    out = shape_of((len(values),) + values[0].shape, values[0].dtype)
    return call(kernel, [out], values, [pltpu.VMEM] * len(values), **order)


def finish_preact(neur, bias, chunks, t, n_neur, width, before=None, **order):
    orders = [rows_of for rows_of, _, _ in chunks]
    ins = [neur, bias]
    for _, own, got in chunks:
        ins += [own] + list(got)
    counts = [len(got) for _, _, got in chunks]
    aliases = {}
    spaces = [pltpu.SMEM] + [pltpu.VMEM] * (len(ins) - 1)
    if before is not None:
        aliases = {len(ins): 0, len(ins) + 1: 1}
        ins += [before[0], before[1]]
        spaces += [pl.ANY, pltpu.VMEM]
    pieces = sum(len(rows_of) for rows_of in orders)

    def kernel(*refs):
        neur_ref, bias_ref = refs[:2]
        relu_ref, target_ref, relu, sems = refs[-4:]
        at, piece, copies = 2, 0, []
        for rows_of, count in zip(orders, counts):
            own_ref, got_refs = refs[at], refs[at + 1 : at + 1 + count]
            at += 1 + count
            for i, s in enumerate(rows_of):
                rows = pl.ds(pl.multiple_of((neur_ref[0] ^ s) * t, t), t)
                here = slice(i * t, (i + 1) * t)
                value = own_ref[here, :] + bias_ref[...]
                for got_ref in got_refs:
                    value = value + got_ref[here, :].astype(f32)
                relu[piece] = jnp.maximum(value, 0.0).astype(bf16)
                copies.append(pltpu.make_async_copy(relu.at[piece], relu_ref.at[rows, :], sems.at[piece]))
                copies[-1].start()
                target_ref[rows, :] = jax.nn.sigmoid(value)
                piece += 1
        for copy in copies:
            copy.wait()

    return call(
        kernel,
        [shape_of((n_neur * t, width), bf16), shape_of((n_neur * t, width), f32)],
        ins,
        spaces,
        scratch=[pltpu.VMEM((pieces, t, width), bf16), pltpu.SemaphoreType.DMA((pieces,))],
        aliases=aliases,
        out_spaces=[pl.ANY, pltpu.VMEM],
        **order,
    )


def hidden_sums(row, shards, down, orders, pairs, t, **order):
    rank = down.shape[1]
    listed = [s for rows_of in orders for s in rows_of]

    def kernel(row_ref, down_ref, *refs):
        keep_ref, send_ref = refs[-2:]
        sums = jnp.dot(joined(refs[: len(listed)]), down_ref[...], preferred_element_type=f32)
        value = {s: sums[i * t : (i + 1) * t, :] for i, s in enumerate(listed)}
        first = row_ref[0] % 2 == 0
        for i, (a, b) in enumerate(pairs):
            keep_ref[i * t : (i + 1) * t, :] = jnp.where(first, value[a], value[b])
            send_ref[i * t : (i + 1) * t, :] = jnp.where(first, value[b], value[a])

    out = shape_of((len(pairs) * t, rank), f32)
    ins = [row, down] + [shards[s] for s in listed]
    return call(kernel, [out, out], ins, [pltpu.SMEM] + [pltpu.VMEM] * (len(ins) - 1), **order)


def assemble_hidden(at, groups, places, lines, t, rank, **order):
    ins, layout = [at], []
    for pairs, mine, theirs in groups:
        for ours, stacks in ((True, mine), (False, theirs)):
            layout.append((pairs, ours, len(ins)))
            ins += stacks
    n_neur = places * lines

    def kernel(*refs):
        at_ref, out_ref = refs[0], refs[-1]
        core, neur = at_ref[0], at_ref[1]
        for pairs, ours, first in layout:
            which = core if ours else 1 - core
            for e in range(lines):
                for d in range(places):
                    owner = neur ^ (d * lines + e)
                    cols = pl.ds(pl.multiple_of(owner * rank, 128), rank)
                    for i, (a, b) in enumerate(pairs):
                        shard = owner ^ (a ^ (which * (a ^ b)))
                        rows = pl.ds(pl.multiple_of(shard * t, t), t)
                        out_ref[rows, cols] = refs[first + e][d, i * t : (i + 1) * t, :]

    return call(
        kernel, [shape_of((n_neur * t, n_neur * rank), bf16)], ins, [pltpu.SMEM] + [pltpu.VMEM] * (len(ins) - 1), **order
    )


def residue_and_back(at, hidden, target, up, places, lines, half_rows, rank, dtype, **order):
    ranks, width = up.shape
    tile = tile_of(width)

    def kernel(at_ref, hidden_ref, target_ref, up_ref, residue_ref, back_ref, total):
        half, neur = at_ref[0], at_ref[1]
        rows = pl.ds(pl.multiple_of(half * half_rows, half_rows), half_rows)
        for k in range(width // tile):
            cols = slice(k * tile, (k + 1) * tile)
            logits = jnp.dot(hidden_ref[rows, :], up_ref[:, cols], preferred_element_type=f32)
            residue = (loss_weight * (jax.nn.sigmoid(logits) - target_ref[rows, cols])).astype(bf16)
            residue_ref[:, cols] = residue
            term = lax.dot_general(
                residue, up_ref[:, cols], (((1,), (1,)), ((), ())), preferred_element_type=f32
            )
            total[...] = term if k == 0 else total[...] + term
        for j in range(places * lines):
            d = neur ^ j
            back_ref[(d % lines) * places + d // lines] = total[:, j * rank : (j + 1) * rank].astype(dtype)

    return call(
        kernel,
        [shape_of((half_rows, width), bf16), shape_of((places * lines, half_rows, rank), dtype)],
        [at, hidden, target, up],
        [pltpu.SMEM, pltpu.VMEM, pltpu.VMEM, pltpu.VMEM],
        scratch=[pltpu.VMEM((half_rows, ranks), f32)],
        mib=24,
        **order,
    )


def add_lines(total, gots, places, **order):
    _, half_rows, rank = total.shape

    def kernel(total_ref, *refs):
        own_ref, away_ref = refs[-2:]
        for d in range(places):
            value = total_ref[d]
            for got_ref in refs[:-2]:
                value = value + got_ref[d].astype(f32)
            if d == 0:
                own_ref[...] = value
            else:
                away_ref[d - 1] = value.astype(bf16)

    return call(
        kernel,
        [shape_of((half_rows, rank), f32), shape_of((places - 1, half_rows, rank), bf16)],
        [total, *gots],
        [pltpu.VMEM] * (1 + len(gots)),
        **order,
    )


def down_gradient(at, shards, mine, theirs, t):
    count = len(shards)
    rows, depth = count * t, shards[0].shape[1]
    half_rows, rank = mine.shape
    tile = tile_of(depth)

    def kernel(at_ref, mine_ref, theirs_ref, *refs):
        out_ref, back, placed = refs[-3:]
        core, neur = at_ref[0], at_ref[1]
        back[pl.ds(pl.multiple_of(core * half_rows, half_rows), half_rows), :] = mine_ref[...].astype(f32)
        back[pl.ds(pl.multiple_of((1 - core) * half_rows, half_rows), half_rows), :] = theirs_ref[...].astype(f32)
        for s in range(count):
            placed[s * t : (s + 1) * t, :] = back[pl.ds(pl.multiple_of((neur ^ s) * t, t), t), :]
        turned = placed[...].T.astype(bf16)
        for k in range(depth // tile):
            cols = slice(k * tile, (k + 1) * tile)
            whole = joined(refs[:count], cols)
            out_ref[cols, :] = jnp.dot(turned, whole, preferred_element_type=f32).T

    return call(
        kernel,
        [shape_of((depth, rank), f32)],
        [at, mine, theirs, *shards],
        [pltpu.SMEM] + [pltpu.VMEM] * (2 + count),
        scratch=[pltpu.VMEM((rows, rank), f32), pltpu.VMEM((rows, rank), f32)],
        mib=16,
    )[0]


def tuned_body(n_rows, n_neur, lines):
    places = n_neur // lines
    pairs_x = n_rows // 2

    def body(tokens, teacher_up, teacher_bias, predictor_down, predictor_up):
        row = lax.axis_index("rows")
        core = row % 2
        neur = lax.axis_index("neur")
        t = tokens.shape[0]
        half_rows = t * n_neur // 2
        width = teacher_up.shape[1] // n_rows
        rank = predictor_down.shape[1]
        row_at = jnp.reshape(row, (1,)).astype(jnp.int32)
        neur_at = jnp.reshape(neur, (1,)).astype(jnp.int32)
        mine_at = jnp.stack([core, neur]).astype(jnp.int32)
        other_at = jnp.stack([1 - core, neur]).astype(jnp.int32)

        def to_core(value):
            return flip(value, "rows", n_rows, 1)

        shards = {}

        orders = [
            [s for s in range(lines)],
            [s for s in range(lines, 2 * lines)] + [d * lines for d in range(2, places)],
            [s for s in range(2 * lines, n_neur) if s % lines],
        ]
        away = list(range(1, pairs_x))
        owns, arrived, got = {}, {}, {}
        (bias_cols,) = bias_part(row_at, teacher_bias, width, after=(neur_at, mine_at, other_at))
        gate = (bias_cols,)

        def sums(chunk, distances, keep, cost=1, through=(), plus=()):
            nonlocal gate
            out = partial_sums(
                row_at,
                [shards[s] for s in orders[chunk]],
                teacher_up,
                width,
                [(d, keep) for d in distances],
                f32 if keep and distances == [0] else bf16,
                gots=[got[chunk, d] for d in distances] if keep else (),
                plus=plus,
                cost=cost,
                after=gate,
                through=through,
            )
            gate = (out[0],)
            for d, part in zip(distances, out):
                if not keep:
                    got[chunk, d] = to_core(part)
                elif d == 0:
                    owns[chunk] = part
                else:
                    arrived.setdefault(chunk, []).append(flip(part, "rows", n_rows, 2 * d))
            return out[len(distances) :]

        def pin(*values):
            nonlocal gate
            token, *values = hold(*values, after=gate)
            gate = (token,)
            return values

        def finish(chunks, before=None, through=()):
            nonlocal gate
            relu, target, *passed = finish_preact(
                neur_at,
                bias_cols,
                [(orders[c], owns[c], arrived[c]) for c in chunks],
                t,
                n_neur,
                width,
                before,
                after=gate,
                through=through,
            )
            gate = (target,)
            return (relu, target), passed

        def hidden_part(chunks):
            nonlocal gate
            pairs = [(orders[c][k], orders[c][k + 1]) for c in chunks for k in range(0, len(orders[c]), 2)]
            keep, send = hidden_sums(
                row_at, shards, predictor_down, [orders[c] for c in chunks], pairs, t, after=gate
            )
            gate = (keep,)
            return keep, send, pairs

        def along_y(d):
            for e in range(1, lines):
                shards[d * lines + e] = flip(shards[d * lines], "neur", n_neur, e)

        first_cost = 10**7
        for d in range(places):
            shards[d * lines] = tokens if d == 0 else flip(tokens, "neur", n_neur, d * lines)
        along_y(0)
        sums(0, away, False, first_cost)
        sums(0, [0], False, first_cost)
        (shards[lines],) = pin(shards[lines])
        along_y(1)
        sums(0, away, True, first_cost)
        sums(0, [0], True, first_cost)
        rest = [d * lines for d in range(2, places)]
        for s, shard in zip(rest, pin(*[shards[s] for s in rest])):
            shards[s] = shard
        for d in range(2, places):
            along_y(d)
        early_keep, early_send, early_pairs = hidden_part([0, 1])
        early_got = to_core(early_send)
        done, _ = finish([0])
        sums(1, away, False)
        sums(1, [0], False)
        sums(1, away, True)
        late_keep, late_send, late_pairs = hidden_part([2])
        late_got = to_core(late_send)
        sums(1, [0], True)
        (mine,) = add_all(f32, (early_keep, early_got), (late_keep, late_got), after=gate)
        gate = (mine,)
        moved = flip(mine, "rows", n_rows, 2)
        sums(2, away, False)
        sums(2, [0], False)
        (moved,) = pin(moved)
        step = 4
        while step < n_rows:
            (mine,) = add_all(f32, (mine, moved))
            moved = flip(mine, "rows", n_rows, step)
            step *= 2
        (mine,) = add_all(bf16, (mine, moved))
        column = [mine] + [flip(mine, "neur", n_neur, d * lines) for d in range(1, places)]
        sums(2, away, True)
        column = pin(*column)
        (stack,) = stacked(column)
        stacks = [stack] + [flip(stack, "neur", n_neur, e) for e in range(1, lines)]
        others = [to_core(part) for part in stacks]
        sums(2, [0], True, through=())
        done, _ = finish([1], done)
        (teacher_relu, target), _ = finish([2], done)
        (hidden,) = assemble_hidden(
            mine_at, [(early_pairs + late_pairs, stacks, others)], places, lines, t, rank, after=gate
        )

        def half_of(at, dtype, after):
            return residue_and_back(
                at, hidden, target, predictor_up, places, lines, half_rows, rank, dtype, after=after
            )

        residue_other, send = half_of(other_at, bf16, ())
        residue_mine, kept_back = half_of(mine_at, f32, (send,))
        total = kept_back + to_core(send)
        gots = [
            flip(total[e * places : (e + 1) * places].astype(bf16), "neur", n_neur, e) for e in range(1, lines)
        ]
        swap = core == 0
        residue = jnp.concatenate(
            [jnp.where(swap, residue_mine, residue_other), jnp.where(swap, residue_other, residue_mine)]
        )
        grad_up = jnp.einsum("tr,tf->rf", hidden, residue, preferred_element_type=f32)
        back, away = add_lines(total[:places], gots, places, after=(grad_up,))
        for d in range(1, places):
            back = back + flip(away[d - 1], "neur", n_neur, d * lines)
        step = 2
        while step < n_rows:
            back = back + flip(back, "rows", n_rows, step)
            step *= 2
        back = back.astype(bf16)
        grad_down = down_gradient(mine_at, [shards[s] for s in range(n_neur)], back, to_core(back), t)
        return (teacher_relu, grad_down, grad_up)

    return body


def solution(mesh):
    in_specs = (
        P("neur", "rows"),
        P("rows", "neur"),
        P("neur"),
        P("rows", "neur"),
        P(None, ("neur", "rows")),
    )
    out_specs = (P(None, ("neur", "rows")), P("rows", "neur"), P(None, ("neur", "rows")))
    n_rows, n_neur = mesh.shape["rows"], mesh.shape["neur"]
    lines = 1
    while lines * lines * 4 <= n_neur:
        lines *= 2
    tuned = tuned_body(n_rows, n_neur, lines)
    general = general_body(n_rows, n_neur)

    def body(tokens, teacher_up, teacher_bias, predictor_down, predictor_up):
        blocks = (teacher_up.shape[1] // n_rows, predictor_down.shape[1], predictor_up.shape[1])
        fits = all(size % 128 == 0 for size in blocks) and tokens.shape[0] % 16 == 0
        small = teacher_up.size * teacher_up.dtype.itemsize <= 40 * 2**20
        chosen = tuned if fits and small else general
        return chosen(tokens, teacher_up, teacher_bias, predictor_down, predictor_up)

    return jax.shard_map(body, mesh=mesh, in_specs=in_specs, out_specs=out_specs, check_vma=False)
```

```python
import jax
import jax.numpy as jnp
from jax import lax
from jax.experimental import pallas as pl
from jax.experimental.pallas import tpu as pltpu
from jax.sharding import PartitionSpec as P

loss_weight = 0.03125
bf16 = jnp.bfloat16
f32 = jnp.float32


def flip(value, axis, size, distance):
    return lax.ppermute(value, axis, [(i, i ^ distance) for i in range(size)])


def block(value, index, width, axis):
    return lax.dynamic_slice_in_dim(value, index * width, width, axis)


def gather_line(own, lines, size, place):
    def pairs(moves):
        return [(a * lines + y, b * lines + y) for a, b in moves for y in range(lines)]

    edge = (place == 0) | (place == 3)
    middle = pairs([(1, 2), (2, 1)])
    outward = pairs([(1, 0), (2, 3)])
    near = flip(own, "neur", size, lines)
    across = lax.ppermute(own, "neur", middle)
    far = lax.ppermute(near, "neur", middle)
    second = jnp.where(edge, lax.ppermute(across, "neur", outward), far)
    third = jnp.where(edge, lax.ppermute(far, "neur", outward), across)
    return [own, near, second, third]


def general_body(n_rows, n_neur):
    lines = 1
    while lines * lines * 4 <= n_neur:
        lines *= 2
    places = n_neur // lines
    pairs_x = n_rows // 2

    def body(tokens, teacher_up, teacher_bias, predictor_down, predictor_up):
        row = lax.axis_index("rows")
        core, x = row % 2, row // 2
        neur = lax.axis_index("neur")
        place, line = neur // lines, neur % lines
        t = tokens.shape[0]
        half_rows = t * n_neur // 2
        width = teacher_up.shape[1] // n_rows
        rank = predictor_down.shape[1]
        ranks = predictor_up.shape[0]

        if places == 4:
            column = gather_line(tokens, lines, n_neur, place)
        else:
            column = [tokens] + [flip(tokens, "neur", n_neur, d * lines) for d in range(1, places)]
        shards = []
        for shard in column:
            shards.append(shard)
            for d in range(1, lines):
                shards.append(flip(shard, "neur", n_neur, d))
        half = n_neur // 2
        within = neur % half
        side = neur // half

        def ordered(parts):
            whole = jnp.zeros((half_rows, tokens.shape[1]), bf16)
            for s, part in enumerate(parts):
                whole = lax.dynamic_update_slice_in_dim(whole, part, (within ^ s) * t, 0)
            return whole

        near_rows = ordered(shards[:half])
        far_rows = ordered(shards[half:])

        def in_order(near, far):
            return jnp.where(side == 0, jnp.concatenate([near, far]), jnp.concatenate([far, near]))

        gathered = in_order(near_rows, far_rows)

        hidden_part = jnp.dot(gathered, predictor_down, preferred_element_type=f32)
        mine = block(hidden_part, core, half_rows, 0)
        mine = mine + flip(block(hidden_part, 1 - core, half_rows, 0), "rows", n_rows, 1)
        step = 2
        while step < n_rows:
            mine = mine + flip(mine, "rows", n_rows, step)
            step *= 2
        mine = mine.astype(bf16)
        column = [mine] + [flip(mine, "neur", n_neur, d * lines) for d in range(1, places)]
        stack = jnp.stack(column)
        stacks = [stack] + [flip(stack, "neur", n_neur, e) for e in range(1, lines)]
        blocks = [stacks[d % lines][d // lines] for d in range(n_neur)]
        hidden_half = jnp.zeros((half_rows, ranks), bf16)
        for d, part in enumerate(blocks):
            hidden_half = lax.dynamic_update_slice_in_dim(hidden_half, part, (neur ^ d) * rank, 1)
        other = flip(hidden_half, "rows", n_rows, 1)
        hidden = jnp.where(
            core == 0,
            jnp.concatenate([hidden_half, other]),
            jnp.concatenate([other, hidden_half]),
        )

        bias_cols = block(teacher_bias, row, width, 0)

        def preactivation(part):
            value = jnp.dot(part, teacher_up, preferred_element_type=f32)
            value = value.reshape(part.shape[0], pairs_x, 2, width)
            keep = lax.dynamic_index_in_dim(value, core, 2, keepdims=False)
            send = lax.dynamic_index_in_dim(value, 1 - core, 2, keepdims=False)
            chip = keep + flip(send.astype(bf16), "rows", n_rows, 1)
            total = lax.dynamic_index_in_dim(chip, x, 1, keepdims=False)
            for d in range(1, pairs_x):
                away = lax.dynamic_index_in_dim(chip, x ^ d, 1, keepdims=False)
                total = total + flip(away.astype(bf16), "rows", n_rows, 2 * d)
            return total + bias_cols[None, :]

        preact = in_order(preactivation(near_rows), preactivation(far_rows))
        teacher_relu = jnp.maximum(preact, 0.0).astype(bf16)
        target = jax.nn.sigmoid(preact)
        logits = jnp.dot(hidden, predictor_up, preferred_element_type=f32)
        residue = (loss_weight * (jax.nn.sigmoid(logits) - target)).astype(bf16)
        grad_up = jnp.einsum("tr,tf->rf", hidden, residue, preferred_element_type=f32)

        back_part = jnp.einsum("tf,rf->tr", residue, predictor_up, preferred_element_type=f32)
        total = block(back_part, core, half_rows, 0)
        total = total + flip(block(back_part, 1 - core, half_rows, 0), "rows", n_rows, 1)
        total = total.reshape(half_rows, places, lines, rank)
        kept = lax.dynamic_index_in_dim(total, line, 2, keepdims=False)
        for e in range(1, lines):
            away = lax.dynamic_index_in_dim(total, line ^ e, 2, keepdims=False)
            kept = kept + flip(away.astype(bf16), "neur", n_neur, e)
        back = lax.dynamic_index_in_dim(kept, place, 1, keepdims=False)
        for d in range(1, places):
            away = lax.dynamic_index_in_dim(kept, place ^ d, 1, keepdims=False)
            back = back + flip(away.astype(bf16), "neur", n_neur, d * lines)
        step = 2
        while step < n_rows:
            back = back + flip(back, "rows", n_rows, step)
            step *= 2
        back = back.astype(bf16)
        other = flip(back, "rows", n_rows, 1)
        back = jnp.where(
            core == 0, jnp.concatenate([back, other]), jnp.concatenate([other, back])
        )
        grad_down = jnp.einsum("td,tr->dr", gathered, back, preferred_element_type=f32)
        return (teacher_relu, grad_down, grad_up)

    return body


def spot(space=pltpu.VMEM):
    return pl.BlockSpec(memory_space=space)


def shape_of(shape, dtype):
    return jax.ShapeDtypeStruct(shape, dtype)


def call(kernel, outs, ins, spaces, scratch=(), mib=12, after=(), through=(), weight=1, aliases=None, out_spaces=None):
    outs = list(outs)
    out_spaces = list(out_spaces or [pltpu.VMEM] * len(outs))
    passed = list(through)
    n_in, n_out = len(ins), len(outs)

    def body(*refs):
        end = n_in + len(passed) + len(after)
        kernel(*refs[:n_in], *refs[end : end + n_out], *refs[end + n_out + len(passed) :])

    places = [pl.ANY] * len(through)
    outs += [shape_of(value.shape, value.dtype) for value in through]
    aliased = dict(aliases or {})
    aliased.update({n_in + k: n_out + k for k in range(len(passed))})
    results = pl.pallas_call(
        body,
        out_shape=tuple(outs),
        in_specs=[spot(space) for space in list(spaces) + places + [pl.ANY] * len(after)],
        out_specs=tuple(spot(space) for space in out_spaces + places),
        scratch_shapes=list(scratch),
        input_output_aliases=aliased,
        compiler_params=pltpu.CompilerParams(vmem_limit_bytes=mib * 2**20),
        cost_estimate=pl.CostEstimate(flops=weight * 10**6, bytes_accessed=1000, transcendentals=0),
    )(*ins, *through, *after)
    return results


def tile_of(width):
    for tile in (512, 384, 256, 128):
        if width % tile == 0:
            return tile
    return width


def held(value):
    return pltpu.with_memory_space_constraint(value, pltpu.VMEM)


def bias_part(row, bias, width, **order):
    def kernel(row_ref, bias_ref, cols_ref):
        cols_ref[...] = bias_ref[:, pl.ds(pl.multiple_of(row_ref[0] * width, 128), width)]

    return call(
        kernel,
        [shape_of((1, width), f32)],
        [row, bias.reshape(1, bias.shape[0])],
        [pltpu.SMEM, pltpu.VMEM],
        **order,
    )


def hold(*values, **order):
    def kernel(out_ref):
        out_ref[...] = jnp.zeros_like(out_ref)

    return call(kernel, [shape_of((8, 128), f32)], [], [], through=values, **order)


def joined(refs, cols=slice(None)):
    return jnp.concatenate([ref[:, cols] for ref in refs]) if len(refs) > 1 else refs[0][:, cols]


def partial_sums(row, parts, weight, width, blocks, gots=None, pieces=None, retain=False, split=1, cost=1, **order):
    rows = sum(part.shape[0] for part in parts)
    depth = weight.shape[0]
    tile = tile_of(width)
    per = width // tile
    tiles = len(blocks) * per
    slots, ahead = min(tiles, 3), min(tiles, 2)
    gots = gots or []
    flat = [part for listed in gots for part in listed]
    splits = [1 if keep else split for _, keep, _ in blocks]
    starts = [sum(splits[:k]) for k in range(len(blocks) + 1)]
    loads = pieces is None
    ins = [row, *parts, *flat] + ([pltpu.with_memory_space_constraint(weight, pltpu.HBM)] if loads else [held(piece) for piece in pieces])
    n_weights = 1 if loads else len(pieces)

    def kernel(*refs):
        row_ref, part_refs = refs[0], refs[1 : 1 + len(parts)]
        got_refs = refs[1 + len(parts) : len(ins) - n_weights]
        weight_refs = refs[len(ins) - n_weights : len(ins)]
        outs = refs[len(ins) : len(ins) + starts[-1]]
        kept = refs[len(ins) + starts[-1] : len(ins) + starts[-1] + len(blocks)] if retain else ()
        x, core = row_ref[0] // 2, row_ref[0] % 2

        def cols_of(j):
            return slice(j % per * tile, (j % per + 1) * tile)

        def tile_ref(j):
            if not loads:
                return weight_refs[j // per].at[:, cols_of(j)]
            return kept[j // per].at[:, cols_of(j)] if retain else refs[-2].at[j % slots]

        def copy(j):
            distance, keep, _ = blocks[j // per]
            whose = (x ^ distance) * 2 + (core if keep else 1 - core)
            from_cols = pl.ds(pl.multiple_of(whose * width + (j % per) * tile, 128), tile)
            return pltpu.make_async_copy(weight_refs[0].at[:, from_cols], tile_ref(j), refs[-1].at[j % slots])

        if loads:
            for j in range(ahead):
                copy(j).start()
        part = joined(part_refs)
        for j in range(tiles):
            if loads:
                copy(j).wait()
                if j + ahead < tiles:
                    copy(j + ahead).start()
            value = jnp.dot(part, tile_ref(j)[...], preferred_element_type=f32)
            b = j // per
            if gots:
                count = len(gots[b])
                value = value + joined(got_refs[b * count : (b + 1) * count], cols_of(j)).astype(f32)
            value = value.astype(blocks[b][2])
            height = rows // splits[b]
            for k in range(splits[b]):
                outs[starts[b] + k][:, cols_of(j)] = value[k * height : (k + 1) * height, :]

    scratch = []
    if loads:
        scratch = [pltpu.VMEM((8, 128) if retain else (slots, depth, tile), bf16), pltpu.SemaphoreType.DMA((slots,))]
    return call(
        kernel,
        [shape_of((rows // n, width), dtype) for n, (_, _, dtype) in zip(splits, blocks) for _ in range(n)]
        + [pltpu.VMEM((depth, width), bf16) for _ in blocks if retain],
        ins,
        [pltpu.SMEM] + [pltpu.VMEM] * (len(ins) - 1 - n_weights) + [pl.ANY if loads else pltpu.VMEM] * n_weights,
        scratch=scratch,
        mib=10 if retain or not loads else 16,
        weight=cost,
        **order,
    )


def add_all(dtype, *groups, **order):
    rows = [group[0].shape[0] for group in groups]

    def kernel(*refs):
        out_ref, at, first = refs[-1], 0, 0
        for group, size in zip(groups, rows):
            value = refs[at][...]
            for k in range(1, len(group)):
                value = value.astype(f32) + refs[at + k][...].astype(f32)
            out_ref[first : first + size, :] = value.astype(dtype)
            at, first = at + len(group), first + size

    ins = [value for group in groups for value in group]
    out = shape_of((sum(rows), groups[0][0].shape[1]), dtype)
    return call(kernel, [out], ins, [pltpu.VMEM] * len(ins), **order)


def stacked(values, flat=False, **order):
    rows, columns = values[0].shape

    def kernel(*refs):
        for k in range(len(values)):
            if flat:
                refs[-1][k * rows : (k + 1) * rows, :] = refs[k][...]
            else:
                refs[-1][k] = refs[k][...]

    shape = (len(values) * rows, columns) if flat else (len(values), rows, columns)
    return call(kernel, [shape_of(shape, values[0].dtype)], values, [pltpu.VMEM] * len(values), **order)


def finish_preact(neur, bias, chunks, t, n_neur, width, before=None, **order):
    orders = [rows_of for rows_of, _, _ in chunks]
    ins = [neur, bias]
    for _, own, got in chunks:
        ins += [own] + list(got)
    counts = [len(got) for _, _, got in chunks]
    aliases = {}
    spaces = [pltpu.SMEM] + [pltpu.VMEM] * (len(ins) - 1)
    if before is not None:
        aliases = {len(ins): 0, len(ins) + 1: 1}
        ins += [before[0], before[1]]
        spaces += [pl.ANY, pltpu.VMEM]
    pieces = sum(len(rows_of) for rows_of in orders)

    def kernel(*refs):
        neur_ref, bias_ref = refs[:2]
        relu_ref, target_ref, relu, sems = refs[-4:]
        at, piece, copies = 2, 0, []
        for rows_of, count in zip(orders, counts):
            own_ref, got_refs = refs[at], refs[at + 1 : at + 1 + count]
            at += 1 + count
            for i, s in enumerate(rows_of):
                rows = pl.ds(pl.multiple_of((neur_ref[0] ^ s) * t, t), t)
                here = slice(i * t, (i + 1) * t)
                value = own_ref[here, :] + bias_ref[...]
                for got_ref in got_refs:
                    value = value + got_ref[here, :].astype(f32)
                relu[piece] = jnp.maximum(value, 0.0).astype(bf16)
                copies.append(pltpu.make_async_copy(relu.at[piece], relu_ref.at[rows, :], sems.at[piece]))
                copies[-1].start()
                target_ref[rows, :] = jax.nn.sigmoid(value)
                piece += 1
        for copy in copies:
            copy.wait()

    return call(
        kernel,
        [shape_of((n_neur * t, width), bf16), shape_of((n_neur * t, width), f32)],
        ins,
        spaces,
        scratch=[pltpu.VMEM((pieces, t, width), bf16), pltpu.SemaphoreType.DMA((pieces,))],
        aliases=aliases,
        out_spaces=[pl.ANY, pltpu.VMEM],
        **order,
    )


def hidden_sums(row, shards, down, orders, pairs, t, **order):
    rank = down.shape[1]
    listed = [s for rows_of in orders for s in rows_of]

    def kernel(row_ref, down_ref, *refs):
        keep_ref, send_ref = refs[-2:]
        sums = jnp.dot(joined(refs[: len(shards)]), down_ref[...], preferred_element_type=f32)
        value = {s: sums[i * t : (i + 1) * t, :] for i, s in enumerate(listed)}
        first = row_ref[0] % 2 == 0
        for i, (a, b) in enumerate(pairs):
            keep_ref[i * t : (i + 1) * t, :] = jnp.where(first, value[a], value[b])
            send_ref[i * t : (i + 1) * t, :] = jnp.where(first, value[b], value[a])

    out = shape_of((len(pairs) * t, rank), f32)
    ins = [row, down, *shards]
    return call(kernel, [out, out], ins, [pltpu.SMEM] + [pltpu.VMEM] * (len(ins) - 1), **order)


def assemble_hidden(at, groups, places, lines, t, rank, **order):
    ins, layout = [at], []
    for pairs, mine, theirs in groups:
        for ours, stacks in ((True, mine), (False, theirs)):
            layout.append((pairs, ours, len(ins)))
            ins += stacks
    n_neur = places * lines

    def kernel(*refs):
        at_ref, out_ref = refs[0], refs[-1]
        core, neur = at_ref[0], at_ref[1]
        for pairs, ours, first in layout:
            which = core if ours else 1 - core
            for e in range(lines):
                for d in range(places):
                    owner = neur ^ (d * lines + e)
                    cols = pl.ds(pl.multiple_of(owner * rank, 128), rank)
                    for i, (a, b) in enumerate(pairs):
                        shard = owner ^ (a ^ (which * (a ^ b)))
                        rows = pl.ds(pl.multiple_of(shard * t, t), t)
                        out_ref[rows, cols] = refs[first + e][d, i * t : (i + 1) * t, :]

    return call(
        kernel, [shape_of((n_neur * t, n_neur * rank), bf16)], ins, [pltpu.SMEM] + [pltpu.VMEM] * (len(ins) - 1), **order
    )


def residue_and_back(at, hidden, target, up, places, lines, half_rows, rank, dtype, before=None, **order):
    ranks, width = up.shape
    tile = tile_of(width)
    ins = [at, hidden, target, up] + ([] if before is None else [before])

    def kernel(*refs):
        at_ref, hidden_ref, target_ref, up_ref = refs[:4]
        residue_ref, back_ref, total = refs[len(ins) :]
        half, neur = at_ref[0], at_ref[1]
        rows = pl.ds(pl.multiple_of(half * half_rows, half_rows), half_rows)
        for k in range(width // tile):
            cols = slice(k * tile, (k + 1) * tile)
            logits = jnp.dot(hidden_ref[rows, :], up_ref[:, cols], preferred_element_type=f32)
            residue = (loss_weight * (jax.nn.sigmoid(logits) - target_ref[rows, cols])).astype(bf16)
            residue_ref[rows, cols] = residue
            term = lax.dot_general(
                residue, up_ref[:, cols], (((1,), (1,)), ((), ())), preferred_element_type=f32
            )
            total[...] = term if k == 0 else total[...] + term
        for j in range(places * lines):
            d = neur ^ j
            back_ref[(d % lines) * places + d // lines] = total[:, j * rank : (j + 1) * rank].astype(dtype)

    return call(
        kernel,
        [shape_of((2 * half_rows, width), bf16), shape_of((places * lines, half_rows, rank), dtype)],
        ins,
        [pltpu.SMEM] + [pltpu.VMEM] * (len(ins) - 1),
        scratch=[pltpu.VMEM((half_rows, ranks), f32)],
        mib=24,
        aliases={} if before is None else {4: 0},
        **order,
    )


def add_lines(kept, got, places, lines, after=()):
    _, half_rows, rank = kept.shape

    def kernel(kept_ref, got_ref, own_ref, *away_refs):
        for d in range(places):
            own_ref[d] = kept_ref[d] + got_ref[d].astype(f32)
            for e, away_ref in enumerate(away_refs):
                k = (e + 1) * places + d
                away_ref[d] = (kept_ref[k] + got_ref[k].astype(f32)).astype(bf16)

    outs = [shape_of((places, half_rows, rank), f32)] + [shape_of((places, half_rows, rank), bf16)] * (lines - 1)
    return call(kernel, outs, [kept, got], [pltpu.VMEM] * 2, after=after)


def add_places(own, gots, places, after=()):
    _, half_rows, rank = own.shape

    def kernel(own_ref, *refs):
        got_refs, outs = refs[: len(gots)], refs[len(gots) :]
        for d in range(places):
            value = own_ref[d]
            for got_ref in got_refs:
                value = value + got_ref[d].astype(f32)
            outs[d][...] = value.astype(f32 if d == 0 else bf16)

    outs = [shape_of((half_rows, rank), f32)] + [shape_of((half_rows, rank), bf16)] * (places - 1)
    return call(kernel, outs, [own, *gots], [pltpu.VMEM] * (1 + len(gots)), after=after)


def down_gradient(at, shards, order, mine, theirs, t):
    count = len(shards)
    rows, depth = len(order) * t, shards[0].shape[1]
    half_rows, rank = mine.shape
    tile = tile_of(depth)

    def kernel(at_ref, mine_ref, theirs_ref, *refs):
        out_ref, back, placed = refs[-3:]
        core, neur = at_ref[0], at_ref[1]
        back[pl.ds(pl.multiple_of(core * half_rows, half_rows), half_rows), :] = mine_ref[...].astype(f32)
        back[pl.ds(pl.multiple_of((1 - core) * half_rows, half_rows), half_rows), :] = theirs_ref[...].astype(f32)
        for i, s in enumerate(order):
            placed[i * t : (i + 1) * t, :] = back[pl.ds(pl.multiple_of((neur ^ s) * t, t), t), :]
        turned = placed[...].T.astype(bf16)
        for k in range(depth // tile):
            cols = slice(k * tile, (k + 1) * tile)
            whole = joined(refs[:count], cols)
            out_ref[cols, :] = jnp.dot(turned, whole, preferred_element_type=f32).T

    return call(
        kernel,
        [shape_of((depth, rank), f32)],
        [at, mine, theirs, *shards],
        [pltpu.SMEM] + [pltpu.VMEM] * (2 + count),
        scratch=[pltpu.VMEM((rows, rank), f32), pltpu.VMEM((rows, rank), f32)],
        mib=16,
    )[0]


def tuned_body(n_rows, n_neur, lines):
    places = n_neur // lines
    pairs_x = n_rows // 2

    def body(tokens, teacher_up, teacher_bias, predictor_down, predictor_up):
        row = lax.axis_index("rows")
        core = row % 2
        neur = lax.axis_index("neur")
        t = tokens.shape[0]
        half_rows = t * n_neur // 2
        width = teacher_up.shape[1] // n_rows
        rank = predictor_down.shape[1]
        row_at = jnp.reshape(row, (1,)).astype(jnp.int32)
        neur_at = jnp.reshape(neur, (1,)).astype(jnp.int32)
        mine_at = jnp.stack([core, neur]).astype(jnp.int32)
        other_at = jnp.stack([1 - core, neur]).astype(jnp.int32)

        def to_core(value):
            return flip(value, "rows", n_rows, 1)

        shards = {}

        orders = [
            [s for s in range(lines)],
            [s for s in range(lines, 2 * lines)],
            [d * lines for d in range(2, places)],
            [d * lines + e for e in range(1, lines) for d in range(2, places)],
        ]
        parts = {}
        away = list(range(1, pairs_x))
        splits = 2
        owns, arrived, got, mine_part, kept = {}, {}, {}, {}, {}
        (bias_cols,) = bias_part(row_at, teacher_bias, width, after=(neur_at, mine_at, other_at))
        gate = (bias_cols,)

        def blocks_of(chunk, distance, keep, cost=1, through=(), wait=False):
            nonlocal gate
            outs = partial_sums(
                row_at,
                parts[chunk],
                teacher_up,
                width,
                [(distance, keep, f32 if keep and distance == 0 else bf16)],
                gots=[got[chunk, distance]] if keep else None,
                pieces=[kept[distance, keep]] if chunk else None,
                retain=chunk == 0,
                split=splits,
                cost=cost,
                after=gate,
                through=through,
            )
            gate = (outs[0],)
            if keep:
                part, *outs = outs
                if distance == 0:
                    owns[chunk] = [part]
                elif wait:
                    outs.append(part)
                else:
                    arrived.setdefault(chunk, []).append(flip(part, "rows", n_rows, 2 * distance))
            else:
                got[chunk, distance] = [to_core(part) for part in outs[:splits]]
                outs = outs[splits:]
            if chunk == 0:
                kept[distance, keep], *outs = outs
            return outs

        def pin(*values, cost=1):
            nonlocal gate
            token, *values = hold(*values, after=gate, weight=cost)
            gate = (token,)
            return values

        def finish(chunks, before=None, through=()):
            nonlocal gate
            relu, target, *passed = finish_preact(
                neur_at,
                bias_cols,
                [(orders[c], owns[c][0], arrived[c]) for c in chunks],
                t,
                n_neur,
                width,
                before,
                after=gate,
                through=through,
            )
            gate = (target,)
            return (relu, target), passed

        def along_y(d):
            for e in range(1, lines):
                shards[d * lines + e] = flip(shards[d * lines], "neur", n_neur, e)

        BIG = 10**4
        shards = [tokens]
        shards += [flip(tokens, "neur", n_neur, e) for e in range(1, lines)]
        near = flip(tokens, "neur", n_neur, lines)
        (later,) = pin(tokens)
        far = [flip(later, "neur", n_neur, d * lines) for d in range(2, places)]
        parts[0] = shards
        for d in away:
            blocks_of(0, d, False, BIG)
        blocks_of(0, 0, False, BIG)
        (near,) = pin(near)
        parts[1] = [near] + [flip(near, "neur", n_neur, e) for e in range(1, lines)]
        for d in away:
            blocks_of(0, d, True, BIG)
        blocks_of(0, 0, True, BIG)
        for d in away:
            blocks_of(1, d, False)
        (far,) = stacked(far, True, after=gate)
        gate = (far,)
        parts[2] = [far]
        parts[3] = [flip(far, "neur", n_neur, e) for e in range(1, lines)]
        blocks_of(1, 0, False)
        for d in away:
            blocks_of(1, d, True)
        for d in away:
            blocks_of(2, d, False)
        done, _ = finish([0])
        blocks_of(1, 0, True)
        blocks_of(2, 0, False)
        for d in away:
            blocks_of(2, d, True)
        blocks_of(2, 0, True)
        done, _ = finish([1], done)
        pairs = [(rows_of[k], rows_of[k + 1]) for rows_of in orders for k in range(0, len(rows_of), 2)]
        hidden_keep, hidden_send = hidden_sums(
            row_at, [part for c in range(4) for part in parts[c]], predictor_down, orders, pairs, t, after=gate
        )
        gate = (hidden_keep,)
        hidden_got = to_core(hidden_send)
        for d in away:
            blocks_of(3, d, False)
        blocks_of(3, 0, False)
        (mine,) = add_all(f32, (hidden_keep, hidden_got), after=gate)
        gate = (mine,)
        moved = flip(mine, "rows", n_rows, 2)
        sends = [blocks_of(3, d, True, wait=True)[-1] for d in away]
        for d, part in zip(away, blocks_of(3, 0, True, through=sends)):
            arrived.setdefault(3, []).append(flip(part, "rows", n_rows, 2 * d))
        done, (moved,) = finish([2], done, [moved])
        step = 4
        while step < n_rows:
            (mine,) = add_all(f32, (mine, moved))
            moved = flip(mine, "rows", n_rows, step)
            step *= 2
        (mine,) = add_all(bf16, (mine, moved), after=gate)
        gate = (mine,)
        column = [mine] + [flip(mine, "neur", n_neur, d * lines) for d in range(1, places)]
        (stack,) = stacked(column, after=gate)
        gate = (stack,)
        stacks = [stack] + [flip(stack, "neur", n_neur, e) for e in range(1, lines)]
        others = [to_core(part) for part in stacks]
        (teacher_relu, target), _ = finish([3], done)
        (hidden,) = assemble_hidden(mine_at, [(pairs, stacks, others)], places, lines, t, rank, after=gate)

        half, send = residue_and_back(
            other_at, hidden, target, predictor_up, places, lines, half_rows, rank, bf16
        )
        residue, kept_back = residue_and_back(
            mine_at, hidden, target, predictor_up, places, lines, half_rows, rank, f32, half
        )
        back, *aways = add_lines(kept_back, to_core(send), places, lines)
        gots = [flip(value, "neur", n_neur, e + 1) for e, value in enumerate(aways)]
        grad_up = jnp.einsum("tr,tf->rf", hidden, residue, preferred_element_type=f32)
        back, *aways = add_places(back, gots, places, after=(grad_up,))
        gots = [flip(value, "neur", n_neur, (d + 1) * lines) for d, value in enumerate(aways)]
        (back,) = add_all(f32, (back, *gots))
        step = 2
        while step < n_rows:
            other = flip(back.astype(bf16), "rows", n_rows, step)
            back = back.astype(bf16).astype(f32) + other
            step *= 2
        back = back.astype(bf16)
        grad_down = down_gradient(
            mine_at, [part for c in range(4) for part in parts[c]], [s for c in orders for s in c], back, to_core(back), t
        )
        return (teacher_relu, grad_down, grad_up)

    return body


def solution(mesh):
    in_specs = (
        P("neur", "rows"),
        P("rows", "neur"),
        P("neur"),
        P("rows", "neur"),
        P(None, ("neur", "rows")),
    )
    out_specs = (P(None, ("neur", "rows")), P("rows", "neur"), P(None, ("neur", "rows")))
    n_rows, n_neur = mesh.shape["rows"], mesh.shape["neur"]
    lines = 1
    while lines * lines * 4 <= n_neur:
        lines *= 2
    tuned = tuned_body(n_rows, n_neur, lines)
    general = general_body(n_rows, n_neur)

    def body(tokens, teacher_up, teacher_bias, predictor_down, predictor_up):
        blocks = (teacher_up.shape[1] // n_rows, predictor_down.shape[1], predictor_up.shape[1])
        fits = all(size % 128 == 0 for size in blocks) and tokens.shape[0] % 16 == 0
        small = teacher_up.size * teacher_up.dtype.itemsize <= 40 * 2**20
        chosen = tuned if fits and small else general
        return chosen(tokens, teacher_up, teacher_bias, predictor_down, predictor_up)

    return jax.shard_map(body, mesh=mesh, in_specs=in_specs, out_specs=out_specs, check_vma=False)
```

```python
import jax
import jax.numpy as jnp
from jax import lax
from jax.experimental import pallas as pl
from jax.experimental.pallas import tpu as pltpu
from jax.sharding import PartitionSpec as P

loss_weight = 0.03125
bf16 = jnp.bfloat16
f32 = jnp.float32


def flip(value, axis, size, distance):
    return lax.ppermute(value, axis, [(i, i ^ distance) for i in range(size)])


def block(value, index, width, axis):
    return lax.dynamic_slice_in_dim(value, index * width, width, axis)


def gather_line(own, lines, size, place):
    def pairs(moves):
        return [(a * lines + y, b * lines + y) for a, b in moves for y in range(lines)]

    edge = (place == 0) | (place == 3)
    middle = pairs([(1, 2), (2, 1)])
    outward = pairs([(1, 0), (2, 3)])
    near = flip(own, "neur", size, lines)
    across = lax.ppermute(own, "neur", middle)
    far = lax.ppermute(near, "neur", middle)
    second = jnp.where(edge, lax.ppermute(across, "neur", outward), far)
    third = jnp.where(edge, lax.ppermute(far, "neur", outward), across)
    return [own, near, second, third]


def general_body(n_rows, n_neur):
    lines = 1
    while lines * lines * 4 <= n_neur:
        lines *= 2
    places = n_neur // lines
    pairs_x = n_rows // 2

    def body(tokens, teacher_up, teacher_bias, predictor_down, predictor_up):
        row = lax.axis_index("rows")
        core, x = row % 2, row // 2
        neur = lax.axis_index("neur")
        place, line = neur // lines, neur % lines
        t = tokens.shape[0]
        half_rows = t * n_neur // 2
        width = teacher_up.shape[1] // n_rows
        rank = predictor_down.shape[1]
        ranks = predictor_up.shape[0]

        if places == 4:
            column = gather_line(tokens, lines, n_neur, place)
        else:
            column = [tokens] + [flip(tokens, "neur", n_neur, d * lines) for d in range(1, places)]
        shards = []
        for shard in column:
            shards.append(shard)
            for d in range(1, lines):
                shards.append(flip(shard, "neur", n_neur, d))
        half = n_neur // 2
        within = neur % half
        side = neur // half

        def ordered(parts):
            whole = jnp.zeros((half_rows, tokens.shape[1]), bf16)
            for s, part in enumerate(parts):
                whole = lax.dynamic_update_slice_in_dim(whole, part, (within ^ s) * t, 0)
            return whole

        near_rows = ordered(shards[:half])
        far_rows = ordered(shards[half:])

        def in_order(near, far):
            return jnp.where(side == 0, jnp.concatenate([near, far]), jnp.concatenate([far, near]))

        gathered = in_order(near_rows, far_rows)

        hidden_part = jnp.dot(gathered, predictor_down, preferred_element_type=f32)
        mine = block(hidden_part, core, half_rows, 0)
        mine = mine + flip(block(hidden_part, 1 - core, half_rows, 0), "rows", n_rows, 1)
        step = 2
        while step < n_rows:
            mine = mine + flip(mine, "rows", n_rows, step)
            step *= 2
        mine = mine.astype(bf16)
        column = [mine] + [flip(mine, "neur", n_neur, d * lines) for d in range(1, places)]
        stack = jnp.stack(column)
        stacks = [stack] + [flip(stack, "neur", n_neur, e) for e in range(1, lines)]
        blocks = [stacks[d % lines][d // lines] for d in range(n_neur)]
        hidden_half = jnp.zeros((half_rows, ranks), bf16)
        for d, part in enumerate(blocks):
            hidden_half = lax.dynamic_update_slice_in_dim(hidden_half, part, (neur ^ d) * rank, 1)
        other = flip(hidden_half, "rows", n_rows, 1)
        hidden = jnp.where(
            core == 0,
            jnp.concatenate([hidden_half, other]),
            jnp.concatenate([other, hidden_half]),
        )

        bias_cols = block(teacher_bias, row, width, 0)

        def preactivation(part):
            value = jnp.dot(part, teacher_up, preferred_element_type=f32)
            value = value.reshape(part.shape[0], pairs_x, 2, width)
            keep = lax.dynamic_index_in_dim(value, core, 2, keepdims=False)
            send = lax.dynamic_index_in_dim(value, 1 - core, 2, keepdims=False)
            chip = keep + flip(send.astype(bf16), "rows", n_rows, 1)
            total = lax.dynamic_index_in_dim(chip, x, 1, keepdims=False)
            for d in range(1, pairs_x):
                away = lax.dynamic_index_in_dim(chip, x ^ d, 1, keepdims=False)
                total = total + flip(away.astype(bf16), "rows", n_rows, 2 * d)
            return total + bias_cols[None, :]

        preact = in_order(preactivation(near_rows), preactivation(far_rows))
        teacher_relu = jnp.maximum(preact, 0.0).astype(bf16)
        target = jax.nn.sigmoid(preact)
        logits = jnp.dot(hidden, predictor_up, preferred_element_type=f32)
        residue = (loss_weight * (jax.nn.sigmoid(logits) - target)).astype(bf16)
        grad_up = jnp.einsum("tr,tf->rf", hidden, residue, preferred_element_type=f32)

        back_part = jnp.einsum("tf,rf->tr", residue, predictor_up, preferred_element_type=f32)
        total = block(back_part, core, half_rows, 0)
        total = total + flip(block(back_part, 1 - core, half_rows, 0), "rows", n_rows, 1)
        total = total.reshape(half_rows, places, lines, rank)
        kept = lax.dynamic_index_in_dim(total, line, 2, keepdims=False)
        for e in range(1, lines):
            away = lax.dynamic_index_in_dim(total, line ^ e, 2, keepdims=False)
            kept = kept + flip(away.astype(bf16), "neur", n_neur, e)
        back = lax.dynamic_index_in_dim(kept, place, 1, keepdims=False)
        for d in range(1, places):
            away = lax.dynamic_index_in_dim(kept, place ^ d, 1, keepdims=False)
            back = back + flip(away.astype(bf16), "neur", n_neur, d * lines)
        step = 2
        while step < n_rows:
            back = back + flip(back, "rows", n_rows, step)
            step *= 2
        back = back.astype(bf16)
        other = flip(back, "rows", n_rows, 1)
        back = jnp.where(
            core == 0, jnp.concatenate([back, other]), jnp.concatenate([other, back])
        )
        grad_down = jnp.einsum("td,tr->dr", gathered, back, preferred_element_type=f32)
        return (teacher_relu, grad_down, grad_up)

    return body


def spot(space=pltpu.VMEM):
    return pl.BlockSpec(memory_space=space)


def shape_of(shape, dtype):
    return jax.ShapeDtypeStruct(shape, dtype)


def call(kernel, outs, ins, spaces, scratch=(), mib=12, after=(), through=(), weight=10**4, aliases=None, out_spaces=None):
    outs = list(outs)
    out_spaces = list(out_spaces or [pltpu.VMEM] * len(outs))
    passed = list(through)
    n_in, n_out = len(ins), len(outs)

    def body(*refs):
        end = n_in + len(passed) + len(after)
        kernel(*refs[:n_in], *refs[end : end + n_out], *refs[end + n_out + len(passed) :])

    places = [pl.ANY] * len(through)
    outs += [shape_of(value.shape, value.dtype) for value in through]
    aliased = dict(aliases or {})
    aliased.update({n_in + k: n_out + k for k in range(len(passed))})
    results = pl.pallas_call(
        body,
        out_shape=tuple(outs),
        in_specs=[spot(space) for space in list(spaces) + places + [pl.ANY] * len(after)],
        out_specs=tuple(spot(space) for space in out_spaces + places),
        scratch_shapes=list(scratch),
        input_output_aliases=aliased,
        compiler_params=pltpu.CompilerParams(vmem_limit_bytes=mib * 2**20),
        cost_estimate=pl.CostEstimate(flops=weight * 10**6, bytes_accessed=1000, transcendentals=0),
    )(*ins, *through, *after)
    return results


def tile_of(width):
    for tile in (512, 384, 256, 128):
        if width % tile == 0:
            return tile
    return width


def held(value):
    return pltpu.with_memory_space_constraint(value, pltpu.VMEM)


def bias_part(row, bias, width, **order):
    def kernel(row_ref, bias_ref, cols_ref):
        cols_ref[...] = bias_ref[:, pl.ds(pl.multiple_of(row_ref[0] * width, 128), width)]

    return call(
        kernel,
        [shape_of((1, width), f32)],
        [row, bias.reshape(1, bias.shape[0])],
        [pltpu.SMEM, pltpu.VMEM],
        **order,
    )


def hold(*values, **order):
    def kernel(out_ref):
        out_ref[...] = jnp.zeros_like(out_ref)

    return call(kernel, [shape_of((8, 128), f32)], [], [], through=values, **order)


def joined(refs, cols=slice(None)):
    return jnp.concatenate([ref[:, cols] for ref in refs]) if len(refs) > 1 else refs[0][:, cols]


def partial_sums(row, parts, weight, width, blocks, gots=None, pieces=None, retain=False, split=1, cost=10**4, **order):
    rows = sum(part.shape[0] for part in parts)
    depth = weight.shape[0]
    tile = tile_of(width)
    per = width // tile
    tiles = len(blocks) * per
    slots, ahead = min(tiles, 3), min(tiles, 2)
    cuts = 4 if depth % 64 == 0 else 1
    gots = gots or []
    flat = [part for listed in gots for part in listed]
    splits = [1 if keep else split for _, keep, _ in blocks]
    starts = [sum(splits[:k]) for k in range(len(blocks) + 1)]
    loads = pieces is None
    ins = [row, *[held(part) for part in parts], *flat] + ([pltpu.with_memory_space_constraint(weight, pltpu.HBM)] if loads else [held(piece) for piece in pieces])
    n_weights = 1 if loads else len(pieces)

    def kernel(*refs):
        row_ref, part_refs = refs[0], refs[1 : 1 + len(parts)]
        got_refs = refs[1 + len(parts) : len(ins) - n_weights]
        weight_refs = refs[len(ins) - n_weights : len(ins)]
        outs = refs[len(ins) : len(ins) + starts[-1]]
        kept = refs[len(ins) + starts[-1] : len(ins) + starts[-1] + len(blocks)] if retain else ()
        x, core = row_ref[0] // 2, row_ref[0] % 2

        def cols_of(j):
            return slice(j % per * tile, (j % per + 1) * tile)

        def tile_ref(j):
            if not loads:
                return weight_refs[j // per].at[:, cols_of(j)]
            return kept[j // per].at[:, cols_of(j)] if retain else refs[-2].at[j % slots]

        def copy(j):
            distance, keep, _ = blocks[j // per]
            whose = (x ^ distance) * 2 + (core if keep else 1 - core)
            from_cols = pl.ds(pl.multiple_of(whose * width + (j % per) * tile, 128), tile)
            return [
                pltpu.make_async_copy(
                    weight_refs[0].at[pl.ds(k * depth // cuts, depth // cuts), from_cols],
                    tile_ref(j).at[pl.ds(k * depth // cuts, depth // cuts), :],
                    refs[-1].at[j % slots, k],
                )
                for k in range(cuts)
            ]

        if loads:
            for j in range(ahead):
                for piece in copy(j):
                    piece.start()
        part = joined(part_refs)
        for j in range(tiles):
            if loads:
                if j + ahead < tiles:
                    for piece in copy(j + ahead):
                        piece.start()
                for piece in copy(j):
                    piece.wait()
            value = jnp.dot(part, tile_ref(j)[...], preferred_element_type=f32)
            b = j // per
            if gots:
                count = len(gots[b])
                value = value + joined(got_refs[b * count : (b + 1) * count], cols_of(j)).astype(f32)
            value = value.astype(blocks[b][2])
            height = rows // splits[b]
            for k in range(splits[b]):
                outs[starts[b] + k][:, cols_of(j)] = value[k * height : (k + 1) * height, :]

    scratch = []
    if loads:
        scratch = [pltpu.VMEM((8, 128) if retain else (slots, depth, tile), bf16), pltpu.SemaphoreType.DMA((slots, cuts))]
    return call(
        kernel,
        [shape_of((rows // n, width), dtype) for n, (_, _, dtype) in zip(splits, blocks) for _ in range(n)]
        + [pltpu.VMEM((depth, width), bf16) for _ in blocks if retain],
        ins,
        [pltpu.SMEM] + [pltpu.VMEM] * (len(ins) - 1 - n_weights) + [pl.ANY if loads else pltpu.VMEM] * n_weights,
        scratch=scratch,
        mib=10 if retain or not loads else 16,
        weight=cost,
        **order,
    )


def add_all(dtype, *groups, **order):
    rows = [group[0].shape[0] for group in groups]

    def kernel(*refs):
        out_ref, at, first = refs[-1], 0, 0
        for group, size in zip(groups, rows):
            value = refs[at][...]
            for k in range(1, len(group)):
                value = value.astype(f32) + refs[at + k][...].astype(f32)
            out_ref[first : first + size, :] = value.astype(dtype)
            at, first = at + len(group), first + size

    ins = [value for group in groups for value in group]
    out = shape_of((sum(rows), groups[0][0].shape[1]), dtype)
    return call(kernel, [out], ins, [pltpu.VMEM] * len(ins), **order)


def stacked(values, flat=False, **order):
    rows, columns = values[0].shape

    def kernel(*refs):
        for k in range(len(values)):
            if flat:
                refs[-1][k * rows : (k + 1) * rows, :] = refs[k][...]
            else:
                refs[-1][k] = refs[k][...]

    shape = (len(values) * rows, columns) if flat else (len(values), rows, columns)
    return call(kernel, [shape_of(shape, values[0].dtype)], values, [pltpu.VMEM] * len(values), **order)


def finish_preact(neur, bias, chunks, t, n_neur, width, before=None, beside=(), **order):
    orders = [rows_of for rows_of, _, _ in chunks]
    ins = [neur, bias]
    for _, own, got in chunks:
        ins += [own] + list(got)
    counts = [len(got) for _, _, got in chunks]
    ins += [held(value) for value in beside]
    aliases = {}
    spaces = [pltpu.SMEM] + [pltpu.VMEM] * (len(ins) - 1)
    if before is not None:
        aliases = {len(ins): 0, len(ins) + 1: 1}
        ins += [before[0], before[1]]
        spaces += [pl.ANY, pltpu.VMEM]
    pieces = sum(len(rows_of) for rows_of in orders)

    def kernel(*refs):
        neur_ref, bias_ref = refs[:2]
        relu_ref, target_ref, relu, sems = refs[-4:]
        at, piece, copies = 2, 0, []
        for rows_of, count in zip(orders, counts):
            own_ref, got_refs = refs[at], refs[at + 1 : at + 1 + count]
            at += 1 + count
            for i, s in enumerate(rows_of):
                rows = pl.ds(pl.multiple_of((neur_ref[0] ^ s) * t, t), t)
                here = slice(i * t, (i + 1) * t)
                value = own_ref[here, :] + bias_ref[...]
                for got_ref in got_refs:
                    value = value + got_ref[here, :].astype(f32)
                relu[piece] = jnp.maximum(value, 0.0).astype(bf16)
                copies.append(pltpu.make_async_copy(relu.at[piece], relu_ref.at[rows, :], sems.at[piece]))
                copies[-1].start()
                target_ref[rows, :] = jax.nn.sigmoid(value)
                piece += 1
        for copy in copies:
            copy.wait()

    return call(
        kernel,
        [shape_of((n_neur * t, width), bf16), shape_of((n_neur * t, width), f32)],
        ins,
        spaces,
        scratch=[pltpu.VMEM((pieces, t, width), bf16), pltpu.SemaphoreType.DMA((pieces,))],
        aliases=aliases,
        out_spaces=[pl.ANY, pltpu.VMEM],
        **order,
    )


def hidden_sums(row, shards, down, orders, pairs, t, **order):
    rank = down.shape[1]
    listed = [s for rows_of in orders for s in rows_of]

    def kernel(row_ref, down_ref, *refs):
        keep_ref, send_ref = refs[-2:]
        sums = jnp.dot(joined(refs[: len(shards)]), down_ref[...], preferred_element_type=f32)
        value = {s: sums[i * t : (i + 1) * t, :] for i, s in enumerate(listed)}
        first = row_ref[0] % 2 == 0
        for i, (a, b) in enumerate(pairs):
            keep_ref[i * t : (i + 1) * t, :] = jnp.where(first, value[a], value[b])
            send_ref[i * t : (i + 1) * t, :] = jnp.where(first, value[b], value[a])

    out = shape_of((len(pairs) * t, rank), f32)
    ins = [row, down, *shards]
    return call(kernel, [out, out], ins, [pltpu.SMEM] + [pltpu.VMEM] * (len(ins) - 1), **order)


def assemble_hidden(at, groups, places, lines, t, rank, **order):
    ins, layout = [at], []
    for pairs, mine, theirs in groups:
        for ours, stacks in ((True, mine), (False, theirs)):
            layout.append((pairs, ours, len(ins)))
            ins += stacks
    n_neur = places * lines

    def kernel(*refs):
        at_ref, out_ref = refs[0], refs[-1]
        core, neur = at_ref[0], at_ref[1]
        for pairs, ours, first in layout:
            which = core if ours else 1 - core
            for e in range(lines):
                for d in range(places):
                    owner = neur ^ (d * lines + e)
                    cols = pl.ds(pl.multiple_of(owner * rank, 128), rank)
                    for i, (a, b) in enumerate(pairs):
                        shard = owner ^ (a ^ (which * (a ^ b)))
                        rows = pl.ds(pl.multiple_of(shard * t, t), t)
                        out_ref[rows, cols] = refs[first + e][d, i * t : (i + 1) * t, :]

    return call(
        kernel, [shape_of((n_neur * t, n_neur * rank), bf16)], ins, [pltpu.SMEM] + [pltpu.VMEM] * (len(ins) - 1), **order
    )


def residue_and_back(at, hidden, target, up, places, lines, half_rows, rank, dtype, before=None, **order):
    ranks, width = up.shape
    tile = tile_of(width)
    ins = [at, hidden, target, up] + ([] if before is None else [before])

    def kernel(*refs):
        at_ref, hidden_ref, target_ref, up_ref = refs[:4]
        residue_ref, back_ref, total = refs[len(ins) :]
        half, neur = at_ref[0], at_ref[1]
        rows = pl.ds(pl.multiple_of(half * half_rows, half_rows), half_rows)
        for k in range(width // tile):
            cols = slice(k * tile, (k + 1) * tile)
            logits = jnp.dot(hidden_ref[rows, :], up_ref[:, cols], preferred_element_type=f32)
            residue = (loss_weight * (jax.nn.sigmoid(logits) - target_ref[rows, cols])).astype(bf16)
            residue_ref[rows, cols] = residue
            term = lax.dot_general(
                residue, up_ref[:, cols], (((1,), (1,)), ((), ())), preferred_element_type=f32
            )
            total[...] = term if k == 0 else total[...] + term
        for j in range(places * lines):
            d = neur ^ j
            back_ref[(d % lines) * places + d // lines] = total[:, j * rank : (j + 1) * rank].astype(dtype)

    return call(
        kernel,
        [shape_of((2 * half_rows, width), bf16), shape_of((places * lines, half_rows, rank), dtype)],
        ins,
        [pltpu.SMEM] + [pltpu.VMEM] * (len(ins) - 1),
        scratch=[pltpu.VMEM((half_rows, ranks), f32)],
        mib=24,
        aliases={} if before is None else {4: 0},
        **order,
    )


def add_lines(kept, got, places, lines, after=()):
    _, half_rows, rank = kept.shape

    def kernel(kept_ref, got_ref, own_ref, *away_refs):
        for d in range(places):
            own_ref[d] = kept_ref[d] + got_ref[d].astype(f32)
            for e, away_ref in enumerate(away_refs):
                k = (e + 1) * places + d
                away_ref[d] = (kept_ref[k] + got_ref[k].astype(f32)).astype(bf16)

    outs = [shape_of((places, half_rows, rank), f32)] + [shape_of((places, half_rows, rank), bf16)] * (lines - 1)
    return call(kernel, outs, [kept, got], [pltpu.VMEM] * 2, after=after)


def add_places(own, gots, places, after=()):
    _, half_rows, rank = own.shape

    def kernel(own_ref, *refs):
        got_refs, outs = refs[: len(gots)], refs[len(gots) :]
        for d in range(places):
            value = own_ref[d]
            for got_ref in got_refs:
                value = value + got_ref[d].astype(f32)
            outs[d][...] = value.astype(f32 if d == 0 else bf16)

    outs = [shape_of((half_rows, rank), f32)] + [shape_of((half_rows, rank), bf16)] * (places - 1)
    return call(kernel, outs, [own, *gots], [pltpu.VMEM] * (1 + len(gots)), after=after)


def down_gradient(at, shards, order, mine, theirs, t):
    count = len(shards)
    rows, depth = len(order) * t, shards[0].shape[1]
    half_rows, rank = mine.shape
    tile = tile_of(depth)

    def kernel(at_ref, mine_ref, theirs_ref, *refs):
        out_ref, back, placed = refs[-3:]
        core, neur = at_ref[0], at_ref[1]
        back[pl.ds(pl.multiple_of(core * half_rows, half_rows), half_rows), :] = mine_ref[...].astype(f32)
        back[pl.ds(pl.multiple_of((1 - core) * half_rows, half_rows), half_rows), :] = theirs_ref[...].astype(f32)
        for i, s in enumerate(order):
            placed[i * t : (i + 1) * t, :] = back[pl.ds(pl.multiple_of((neur ^ s) * t, t), t), :]
        turned = placed[...].T.astype(bf16)
        for k in range(depth // tile):
            cols = slice(k * tile, (k + 1) * tile)
            whole = joined(refs[:count], cols)
            out_ref[cols, :] = jnp.dot(turned, whole, preferred_element_type=f32).T

    return call(
        kernel,
        [shape_of((depth, rank), f32)],
        [at, mine, theirs, *[held(shard) for shard in shards]],
        [pltpu.SMEM] + [pltpu.VMEM] * (2 + count),
        scratch=[pltpu.VMEM((rows, rank), f32), pltpu.VMEM((rows, rank), f32)],
        mib=16,
    )[0]


def tuned_body(n_rows, n_neur, lines):
    places = n_neur // lines
    pairs_x = n_rows // 2

    def body(tokens, teacher_up, teacher_bias, predictor_down, predictor_up):
        row = lax.axis_index("rows")
        core = row % 2
        neur = lax.axis_index("neur")
        t = tokens.shape[0]
        half_rows = t * n_neur // 2
        width = teacher_up.shape[1] // n_rows
        rank = predictor_down.shape[1]
        row_at = jnp.reshape(row, (1,)).astype(jnp.int32)
        neur_at = jnp.reshape(neur, (1,)).astype(jnp.int32)
        mine_at = jnp.stack([core, neur]).astype(jnp.int32)
        other_at = jnp.stack([1 - core, neur]).astype(jnp.int32)

        def to_core(value):
            return flip(value, "rows", n_rows, 1)

        shards = {}

        orders = [
            [s for s in range(lines)],
            [s for s in range(lines, 2 * lines)],
            [d * lines for d in range(2, places)],
            [d * lines + e for e in range(1, lines) for d in range(2, places)],
        ]
        parts = {}
        away = list(range(1, pairs_x))
        splits = 1
        owns, arrived, got, mine_part, kept = {}, {}, {}, {}, {}
        (bias_cols,) = bias_part(row_at, teacher_bias, width, after=(neur_at, mine_at, other_at))
        gate = (bias_cols,)

        def blocks_of(chunk, distance, keep, cost=10**4, through=(), wait=False):
            nonlocal gate
            outs = partial_sums(
                row_at,
                parts[chunk],
                teacher_up,
                width,
                [(distance, keep, f32 if keep and distance == 0 else bf16)],
                gots=[got[chunk, distance]] if keep else None,
                pieces=[kept[distance, keep]] if chunk else None,
                retain=chunk == 0,
                split=splits,
                cost=cost,
                after=gate,
                through=through,
            )
            gate = (outs[0],)
            if keep:
                part, *outs = outs
                if distance == 0:
                    owns[chunk] = [part]
                elif wait:
                    outs.append(part)
                else:
                    arrived.setdefault(chunk, []).append(flip(part, "rows", n_rows, 2 * distance))
            else:
                got[chunk, distance] = [to_core(part) for part in outs[:splits]]
                outs = outs[splits:]
            if chunk == 0:
                kept[distance, keep], *outs = outs
            return outs

        def pin(*values, cost=10**4):
            nonlocal gate
            token, *values = hold(*values, after=gate, weight=cost)
            gate = (token,)
            return values

        def finish(chunks, before=None, through=(), beside=()):
            nonlocal gate
            relu, target, *passed = finish_preact(
                neur_at,
                bias_cols,
                [(orders[c], owns[c][0], arrived[c]) for c in chunks],
                t,
                n_neur,
                width,
                before,
                beside,
                after=gate,
                through=through,
            )
            gate = (target,)
            return (relu, target), passed

        def along_y(d):
            for e in range(1, lines):
                shards[d * lines + e] = flip(shards[d * lines], "neur", n_neur, e)

        BIG = 10**4
        shards = [tokens]
        shards += [flip(tokens, "neur", n_neur, e) for e in range(1, lines)]
        near = flip(tokens, "neur", n_neur, lines)
        far = [flip(tokens, "neur", n_neur, d * lines) for d in range(2, places)]
        parts[0] = shards
        for d in away:
            blocks_of(0, d, False, BIG)
        blocks_of(0, 0, False, BIG)
        (near,) = pin(near)
        parts[1] = [near] + [flip(near, "neur", n_neur, e) for e in range(1, lines)]
        for d in away:
            blocks_of(0, d, True, BIG)
        blocks_of(0, 0, True, BIG)
        for d in away:
            blocks_of(1, d, False)
        (far,) = stacked(far, True, after=gate)
        gate = (far,)
        parts[2] = [far]
        parts[3] = [flip(far, "neur", n_neur, e) for e in range(1, lines)]
        blocks_of(1, 0, False)
        for d in away:
            blocks_of(1, d, True)
        for d in away:
            blocks_of(2, d, False)
        done, _ = finish([0])
        blocks_of(1, 0, True)
        blocks_of(2, 0, False)
        for d in away:
            blocks_of(2, d, True)
        blocks_of(2, 0, True)
        pairs = [(rows_of[k], rows_of[k + 1]) for rows_of in orders for k in range(0, len(rows_of), 2)]
        hidden_keep, hidden_send = hidden_sums(
            row_at, [part for c in range(4) for part in parts[c]], predictor_down, orders, pairs, t, after=gate
        )
        gate = (hidden_keep,)
        hidden_got = to_core(hidden_send)
        done, _ = finish([1], done)
        for d in away:
            blocks_of(3, d, False)
        blocks_of(3, 0, False)
        (mine,) = add_all(f32, (hidden_keep, hidden_got), after=gate)
        gate = (mine,)
        moved = flip(mine, "rows", n_rows, 2)
        sends = [blocks_of(3, d, True, wait=True)[-1] for d in away]
        for d, part in zip(away, blocks_of(3, 0, True, through=sends)):
            arrived.setdefault(3, []).append(flip(part, "rows", n_rows, 2 * d))
        (moved,) = pin(moved)
        step = 4
        while step < n_rows:
            (mine,) = add_all(f32, (mine, moved))
            moved = flip(mine, "rows", n_rows, step)
            step *= 2
        (mine,) = add_all(bf16, (mine, moved), after=gate)
        gate = (mine,)
        column = [mine] + [flip(mine, "neur", n_neur, d * lines) for d in range(1, places)]
        done, _ = finish([2], done)
        (stack,) = stacked(column, after=gate)
        gate = (stack,)
        stacks = [stack] + [flip(stack, "neur", n_neur, e) for e in range(1, lines)]
        others = [to_core(part) for part in stacks]
        (teacher_relu, target), _ = finish([3], done, beside=[predictor_up])
        (hidden,) = assemble_hidden(mine_at, [(pairs, stacks, others)], places, lines, t, rank, after=gate)

        half, send = residue_and_back(
            other_at, hidden, target, predictor_up, places, lines, half_rows, rank, bf16
        )
        residue, kept_back = residue_and_back(
            mine_at, hidden, target, predictor_up, places, lines, half_rows, rank, f32, half
        )
        back, *aways = add_lines(kept_back, to_core(send), places, lines)
        gots = [flip(value, "neur", n_neur, e + 1) for e, value in enumerate(aways)]
        grad_up = jnp.einsum("tr,tf->rf", hidden, residue, preferred_element_type=f32)
        back, *aways = add_places(back, gots, places, after=(grad_up,))
        gots = [flip(value, "neur", n_neur, (d + 1) * lines) for d, value in enumerate(aways)]
        (back,) = add_all(f32, (back, *gots))
        step = 2
        while step < n_rows:
            other = flip(back.astype(bf16), "rows", n_rows, step)
            back = back.astype(bf16).astype(f32) + other
            step *= 2
        back = back.astype(bf16)
        grad_down = down_gradient(
            mine_at, [part for c in range(4) for part in parts[c]], [s for c in orders for s in c], back, to_core(back), t
        )
        return (teacher_relu, grad_down, grad_up)

    return body


def solution(mesh):
    in_specs = (
        P("neur", "rows"),
        P("rows", "neur"),
        P("neur"),
        P("rows", "neur"),
        P(None, ("neur", "rows")),
    )
    out_specs = (P(None, ("neur", "rows")), P("rows", "neur"), P(None, ("neur", "rows")))
    n_rows, n_neur = mesh.shape["rows"], mesh.shape["neur"]
    lines = 1
    while lines * lines * 4 <= n_neur:
        lines *= 2
    tuned = tuned_body(n_rows, n_neur, lines)
    general = general_body(n_rows, n_neur)

    def body(tokens, teacher_up, teacher_bias, predictor_down, predictor_up):
        blocks = (teacher_up.shape[1] // n_rows, predictor_down.shape[1], predictor_up.shape[1])
        fits = all(size % 128 == 0 for size in blocks) and tokens.shape[0] % 16 == 0
        small = teacher_up.size * teacher_up.dtype.itemsize <= 40 * 2**20
        chosen = tuned if fits and small else general
        return chosen(tokens, teacher_up, teacher_bias, predictor_down, predictor_up)

    return jax.shard_map(body, mesh=mesh, in_specs=in_specs, out_specs=out_specs, check_vma=False)
```

```python
import jax
import jax.numpy as jnp
from jax import lax
from jax.experimental import pallas as pl
from jax.experimental.pallas import tpu as pltpu
from jax.sharding import PartitionSpec as P

loss_weight = 0.03125
bf16 = jnp.bfloat16
f32 = jnp.float32


def flip(value, axis, size, distance):
    return lax.ppermute(value, axis, [(i, i ^ distance) for i in range(size)])


def block(value, index, width, axis):
    return lax.dynamic_slice_in_dim(value, index * width, width, axis)


def gather_line(own, lines, size, place):
    def pairs(moves):
        return [(a * lines + y, b * lines + y) for a, b in moves for y in range(lines)]

    edge = (place == 0) | (place == 3)
    middle = pairs([(1, 2), (2, 1)])
    outward = pairs([(1, 0), (2, 3)])
    near = flip(own, "neur", size, lines)
    across = lax.ppermute(own, "neur", middle)
    far = lax.ppermute(near, "neur", middle)
    second = jnp.where(edge, lax.ppermute(across, "neur", outward), far)
    third = jnp.where(edge, lax.ppermute(far, "neur", outward), across)
    return [own, near, second, third]


def general_body(n_rows, n_neur):
    lines = 1
    while lines * lines * 4 <= n_neur:
        lines *= 2
    places = n_neur // lines
    pairs_x = n_rows // 2

    def body(tokens, teacher_up, teacher_bias, predictor_down, predictor_up):
        row = lax.axis_index("rows")
        core, x = row % 2, row // 2
        neur = lax.axis_index("neur")
        place, line = neur // lines, neur % lines
        t = tokens.shape[0]
        half_rows = t * n_neur // 2
        width = teacher_up.shape[1] // n_rows
        rank = predictor_down.shape[1]
        ranks = predictor_up.shape[0]

        if places == 4:
            column = gather_line(tokens, lines, n_neur, place)
        else:
            column = [tokens] + [flip(tokens, "neur", n_neur, d * lines) for d in range(1, places)]
        shards = []
        for shard in column:
            shards.append(shard)
            for d in range(1, lines):
                shards.append(flip(shard, "neur", n_neur, d))
        half = n_neur // 2
        within = neur % half
        side = neur // half

        def ordered(parts):
            whole = jnp.zeros((half_rows, tokens.shape[1]), bf16)
            for s, part in enumerate(parts):
                whole = lax.dynamic_update_slice_in_dim(whole, part, (within ^ s) * t, 0)
            return whole

        near_rows = ordered(shards[:half])
        far_rows = ordered(shards[half:])

        def in_order(near, far):
            return jnp.where(side == 0, jnp.concatenate([near, far]), jnp.concatenate([far, near]))

        gathered = in_order(near_rows, far_rows)

        hidden_part = jnp.dot(gathered, predictor_down, preferred_element_type=f32)
        mine = block(hidden_part, core, half_rows, 0)
        mine = mine + flip(block(hidden_part, 1 - core, half_rows, 0), "rows", n_rows, 1)
        step = 2
        while step < n_rows:
            mine = mine + flip(mine, "rows", n_rows, step)
            step *= 2
        mine = mine.astype(bf16)
        column = [mine] + [flip(mine, "neur", n_neur, d * lines) for d in range(1, places)]
        own_lines = [flip(mine, "neur", n_neur, e) for e in range(1, lines)]
        stack = jnp.stack(column)
        stacks = [stack] + [flip(stack, "neur", n_neur, e) for e in range(1, lines)]
        blocks = [stacks[d % lines][d // lines] for d in range(n_neur)]
        hidden_half = jnp.zeros((half_rows, ranks), bf16)
        for d, part in enumerate(blocks):
            hidden_half = lax.dynamic_update_slice_in_dim(hidden_half, part, (neur ^ d) * rank, 1)
        other = flip(hidden_half, "rows", n_rows, 1)
        hidden = jnp.where(
            core == 0,
            jnp.concatenate([hidden_half, other]),
            jnp.concatenate([other, hidden_half]),
        )

        bias_cols = block(teacher_bias, row, width, 0)

        def preactivation(part):
            value = jnp.dot(part, teacher_up, preferred_element_type=f32)
            value = value.reshape(part.shape[0], pairs_x, 2, width)
            keep = lax.dynamic_index_in_dim(value, core, 2, keepdims=False)
            send = lax.dynamic_index_in_dim(value, 1 - core, 2, keepdims=False)
            chip = keep + flip(send.astype(bf16), "rows", n_rows, 1)
            total = lax.dynamic_index_in_dim(chip, x, 1, keepdims=False)
            for d in range(1, pairs_x):
                away = lax.dynamic_index_in_dim(chip, x ^ d, 1, keepdims=False)
                total = total + flip(away.astype(bf16), "rows", n_rows, 2 * d)
            return total + bias_cols[None, :]

        preact = in_order(preactivation(near_rows), preactivation(far_rows))
        teacher_relu = jnp.maximum(preact, 0.0).astype(bf16)
        target = jax.nn.sigmoid(preact)
        logits = jnp.dot(hidden, predictor_up, preferred_element_type=f32)
        residue = (loss_weight * (jax.nn.sigmoid(logits) - target)).astype(bf16)
        grad_up = jnp.einsum("tr,tf->rf", hidden, residue, preferred_element_type=f32)

        back_part = jnp.einsum("tf,rf->tr", residue, predictor_up, preferred_element_type=f32)
        total = block(back_part, core, half_rows, 0)
        total = total + flip(block(back_part, 1 - core, half_rows, 0), "rows", n_rows, 1)
        total = total.reshape(half_rows, places, lines, rank)
        kept = lax.dynamic_index_in_dim(total, line, 2, keepdims=False)
        for e in range(1, lines):
            away = lax.dynamic_index_in_dim(total, line ^ e, 2, keepdims=False)
            kept = kept + flip(away.astype(bf16), "neur", n_neur, e)
        back = lax.dynamic_index_in_dim(kept, place, 1, keepdims=False)
        for d in range(1, places):
            away = lax.dynamic_index_in_dim(kept, place ^ d, 1, keepdims=False)
            back = back + flip(away.astype(bf16), "neur", n_neur, d * lines)
        step = 2
        while step < n_rows:
            back = back + flip(back, "rows", n_rows, step)
            step *= 2
        back = back.astype(bf16)
        other = flip(back, "rows", n_rows, 1)
        back = jnp.where(
            core == 0, jnp.concatenate([back, other]), jnp.concatenate([other, back])
        )
        grad_down = jnp.einsum("td,tr->dr", gathered, back, preferred_element_type=f32)
        return (teacher_relu, grad_down, grad_up)

    return body


def spot(space=pltpu.VMEM):
    return pl.BlockSpec(memory_space=space)


def shape_of(shape, dtype):
    return jax.ShapeDtypeStruct(shape, dtype)


def call(kernel, outs, ins, spaces, scratch=(), mib=12, after=(), through=(), weight=10**4, aliases=None, out_spaces=None):
    outs = list(outs)
    out_spaces = list(out_spaces or [pltpu.VMEM] * len(outs))
    passed = list(through)
    n_in, n_out = len(ins), len(outs)

    def body(*refs):
        end = n_in + len(passed) + len(after)
        kernel(*refs[:n_in], *refs[end : end + n_out], *refs[end + n_out + len(passed) :])

    places = [pl.ANY] * len(through)
    outs += [shape_of(value.shape, value.dtype) for value in through]
    aliased = dict(aliases or {})
    aliased.update({n_in + k: n_out + k for k in range(len(passed))})
    results = pl.pallas_call(
        body,
        out_shape=tuple(outs),
        in_specs=[spot(space) for space in list(spaces) + places + [pl.ANY] * len(after)],
        out_specs=tuple(spot(space) for space in out_spaces + places),
        scratch_shapes=list(scratch),
        input_output_aliases=aliased,
        compiler_params=pltpu.CompilerParams(vmem_limit_bytes=mib * 2**20),
        cost_estimate=pl.CostEstimate(flops=weight * 10**6, bytes_accessed=1000, transcendentals=0),
    )(*ins, *through, *after)
    return results


def tile_of(width):
    for tile in (512, 384, 256, 128):
        if width % tile == 0:
            return tile
    return width


def held(value):
    return pltpu.with_memory_space_constraint(value, pltpu.VMEM)


def bias_part(row, bias, width, **order):
    def kernel(row_ref, bias_ref, cols_ref):
        cols_ref[...] = bias_ref[:, pl.ds(pl.multiple_of(row_ref[0] * width, 128), width)]

    return call(
        kernel,
        [shape_of((1, width), f32)],
        [row, bias.reshape(1, bias.shape[0])],
        [pltpu.SMEM, pltpu.VMEM],
        **order,
    )


def hold(*values, **order):
    def kernel(out_ref):
        out_ref[...] = jnp.zeros_like(out_ref)

    return call(kernel, [shape_of((8, 128), f32)], [], [], through=values, **order)


def joined(refs, cols=slice(None)):
    return jnp.concatenate([ref[:, cols] for ref in refs]) if len(refs) > 1 else refs[0][:, cols]


def partial_sums(row, parts, weight, width, blocks, gots=None, pieces=None, retain=False, split=1, cost=10**4, **order):
    rows = sum(part.shape[0] for part in parts)
    depth = weight.shape[0]
    tile = tile_of(width)
    per = width // tile
    tiles = len(blocks) * per
    slots, ahead = min(tiles, 3), min(tiles, 2)
    cuts = 4 if depth % 64 == 0 else 1
    gots = gots or []
    flat = [part for listed in gots for part in listed]
    splits = [1 if keep else split for _, keep, _ in blocks]
    starts = [sum(splits[:k]) for k in range(len(blocks) + 1)]
    loads = pieces is None
    ins = [row, *[held(part) for part in parts], *flat] + ([pltpu.with_memory_space_constraint(weight, pltpu.HBM)] if loads else [held(piece) for piece in pieces])
    n_weights = 1 if loads else len(pieces)

    def kernel(*refs):
        row_ref, part_refs = refs[0], refs[1 : 1 + len(parts)]
        got_refs = refs[1 + len(parts) : len(ins) - n_weights]
        weight_refs = refs[len(ins) - n_weights : len(ins)]
        outs = refs[len(ins) : len(ins) + starts[-1]]
        kept = refs[len(ins) + starts[-1] : len(ins) + starts[-1] + len(blocks)] if retain else ()
        x, core = row_ref[0] // 2, row_ref[0] % 2

        def cols_of(j):
            return slice(j % per * tile, (j % per + 1) * tile)

        def tile_ref(j):
            if not loads:
                return weight_refs[j // per].at[:, cols_of(j)]
            return kept[j // per].at[:, cols_of(j)] if retain else refs[-2].at[j % slots]

        def copy(j):
            distance, keep, _ = blocks[j // per]
            whose = (x ^ distance) * 2 + (core if keep else 1 - core)
            from_cols = pl.ds(pl.multiple_of(whose * width + (j % per) * tile, 128), tile)
            return [
                pltpu.make_async_copy(
                    weight_refs[0].at[pl.ds(k * depth // cuts, depth // cuts), from_cols],
                    tile_ref(j).at[pl.ds(k * depth // cuts, depth // cuts), :],
                    refs[-1].at[j % slots, k],
                )
                for k in range(cuts)
            ]

        if loads:
            for j in range(ahead):
                for piece in copy(j):
                    piece.start()
        part = joined(part_refs)
        for j in range(tiles):
            if loads:
                if j + ahead < tiles:
                    for piece in copy(j + ahead):
                        piece.start()
                for piece in copy(j):
                    piece.wait()
            value = jnp.dot(part, tile_ref(j)[...], preferred_element_type=f32)
            b = j // per
            if gots:
                count = len(gots[b])
                value = value + joined(got_refs[b * count : (b + 1) * count], cols_of(j)).astype(f32)
            value = value.astype(blocks[b][2])
            height = rows // splits[b]
            for k in range(splits[b]):
                outs[starts[b] + k][:, cols_of(j)] = value[k * height : (k + 1) * height, :]

    scratch = []
    if loads:
        scratch = [pltpu.VMEM((8, 128) if retain else (slots, depth, tile), bf16), pltpu.SemaphoreType.DMA((slots, cuts))]
    return call(
        kernel,
        [shape_of((rows // n, width), dtype) for n, (_, _, dtype) in zip(splits, blocks) for _ in range(n)]
        + [pltpu.VMEM((depth, width), bf16) for _ in blocks if retain],
        ins,
        [pltpu.SMEM] + [pltpu.VMEM] * (len(ins) - 1 - n_weights) + [pl.ANY if loads else pltpu.VMEM] * n_weights,
        scratch=scratch,
        mib=10 if retain or not loads else 16,
        weight=cost,
        **order,
    )


def add_all(dtype, *groups, **order):
    rows = [group[0].shape[0] for group in groups]

    def kernel(*refs):
        out_ref, at, first = refs[-1], 0, 0
        for group, size in zip(groups, rows):
            value = refs[at][...]
            for k in range(1, len(group)):
                value = value.astype(f32) + refs[at + k][...].astype(f32)
            out_ref[first : first + size, :] = value.astype(dtype)
            at, first = at + len(group), first + size

    ins = [value for group in groups for value in group]
    out = shape_of((sum(rows), groups[0][0].shape[1]), dtype)
    return call(kernel, [out], ins, [pltpu.VMEM] * len(ins), **order)


def stacked(values, flat=False, **order):
    rows, columns = values[0].shape

    def kernel(*refs):
        for k in range(len(values)):
            if flat:
                refs[-1][k * rows : (k + 1) * rows, :] = refs[k][...]
            else:
                refs[-1][k] = refs[k][...]

    shape = (len(values) * rows, columns) if flat else (len(values), rows, columns)
    return call(kernel, [shape_of(shape, values[0].dtype)], values, [pltpu.VMEM] * len(values), **order)


def finish_preact(neur, bias, chunks, t, n_neur, width, before=None, beside=(), **order):
    orders = [rows_of for rows_of, _, _ in chunks]
    ins = [neur, bias]
    for _, own, got in chunks:
        ins += [own] + list(got)
    counts = [len(got) for _, _, got in chunks]
    ins += [held(value) for value in beside]
    aliases = {}
    spaces = [pltpu.SMEM] + [pltpu.VMEM] * (len(ins) - 1)
    if before is not None:
        aliases = {len(ins): 0, len(ins) + 1: 1}
        ins += [before[0], before[1]]
        spaces += [pl.ANY, pltpu.VMEM]
    pieces = sum(len(rows_of) for rows_of in orders)

    def kernel(*refs):
        neur_ref, bias_ref = refs[:2]
        relu_ref, target_ref, relu, sems = refs[-4:]
        at, piece, copies = 2, 0, []
        for rows_of, count in zip(orders, counts):
            own_ref, got_refs = refs[at], refs[at + 1 : at + 1 + count]
            at += 1 + count
            for i, s in enumerate(rows_of):
                rows = pl.ds(pl.multiple_of((neur_ref[0] ^ s) * t, t), t)
                here = slice(i * t, (i + 1) * t)
                value = own_ref[here, :] + bias_ref[...]
                for got_ref in got_refs:
                    value = value + got_ref[here, :].astype(f32)
                relu[piece] = jnp.maximum(value, 0.0).astype(bf16)
                copies.append(pltpu.make_async_copy(relu.at[piece], relu_ref.at[rows, :], sems.at[piece]))
                copies[-1].start()
                target_ref[rows, :] = jax.nn.sigmoid(value)
                piece += 1
        for copy in copies:
            copy.wait()

    return call(
        kernel,
        [shape_of((n_neur * t, width), bf16), shape_of((n_neur * t, width), f32)],
        ins,
        spaces,
        scratch=[pltpu.VMEM((pieces, t, width), bf16), pltpu.SemaphoreType.DMA((pieces,))],
        aliases=aliases,
        out_spaces=[pl.ANY, pltpu.VMEM],
        **order,
    )


def hidden_sums(row, shards, down, orders, pairs, t, **order):
    rank = down.shape[1]
    listed = [s for rows_of in orders for s in rows_of]

    def kernel(row_ref, down_ref, *refs):
        keep_ref, send_ref = refs[-2:]
        sums = jnp.dot(joined(refs[: len(shards)]), down_ref[...], preferred_element_type=f32)
        value = {s: sums[i * t : (i + 1) * t, :] for i, s in enumerate(listed)}
        first = row_ref[0] % 2 == 0
        for i, (a, b) in enumerate(pairs):
            keep_ref[i * t : (i + 1) * t, :] = jnp.where(first, value[a], value[b])
            send_ref[i * t : (i + 1) * t, :] = jnp.where(first, value[b], value[a])

    out = shape_of((len(pairs) * t, rank), f32)
    ins = [row, down, *shards]
    return call(kernel, [out, out], ins, [pltpu.SMEM] + [pltpu.VMEM] * (len(ins) - 1), **order)


def assemble_hidden(at, groups, places, lines, t, rank, **order):
    ins, layout = [at], []
    for pairs, mine, theirs in groups:
        for ours, stacks in ((True, mine), (False, theirs)):
            layout.append((pairs, ours, len(ins)))
            ins += stacks
    n_neur = places * lines

    def kernel(*refs):
        at_ref, out_ref = refs[0], refs[-1]
        core, neur = at_ref[0], at_ref[1]
        for pairs, ours, first in layout:
            which = core if ours else 1 - core
            for e in range(lines):
                for d in range(places):
                    owner = neur ^ (d * lines + e)
                    cols = pl.ds(pl.multiple_of(owner * rank, 128), rank)
                    for i, (a, b) in enumerate(pairs):
                        shard = owner ^ (a ^ (which * (a ^ b)))
                        rows = pl.ds(pl.multiple_of(shard * t, t), t)
                        here = slice(i * t, (i + 1) * t)
                        if d == 0:
                            out_ref[rows, cols] = refs[first + 2 * e][here, :]
                        else:
                            out_ref[rows, cols] = refs[first + 2 * e + 1][d - 1, here, :]

    return call(
        kernel, [shape_of((n_neur * t, n_neur * rank), bf16)], ins, [pltpu.SMEM] + [pltpu.VMEM] * (len(ins) - 1), **order
    )


def residue_and_back(at, hidden, target, up, places, lines, half_rows, rank, dtype, before=None, **order):
    ranks, width = up.shape
    tile = tile_of(width)
    ins = [at, hidden, target, up] + ([] if before is None else [before])

    def kernel(*refs):
        at_ref, hidden_ref, target_ref, up_ref = refs[:4]
        residue_ref, back_ref, total = refs[len(ins) :]
        half, neur = at_ref[0], at_ref[1]
        rows = pl.ds(pl.multiple_of(half * half_rows, half_rows), half_rows)
        for k in range(width // tile):
            cols = slice(k * tile, (k + 1) * tile)
            logits = jnp.dot(hidden_ref[rows, :], up_ref[:, cols], preferred_element_type=f32)
            residue = (loss_weight * (jax.nn.sigmoid(logits) - target_ref[rows, cols])).astype(bf16)
            residue_ref[rows, cols] = residue
            term = lax.dot_general(
                residue, up_ref[:, cols], (((1,), (1,)), ((), ())), preferred_element_type=f32
            )
            total[...] = term if k == 0 else total[...] + term
        for j in range(places * lines):
            d = neur ^ j
            back_ref[(d % lines) * places + d // lines] = total[:, j * rank : (j + 1) * rank].astype(dtype)

    return call(
        kernel,
        [shape_of((2 * half_rows, width), bf16), shape_of((places * lines, half_rows, rank), dtype)],
        ins,
        [pltpu.SMEM] + [pltpu.VMEM] * (len(ins) - 1),
        scratch=[pltpu.VMEM((half_rows, ranks), f32)],
        mib=24,
        aliases={} if before is None else {4: 0},
        **order,
    )


def add_lines(kept, got, places, lines, after=()):
    _, half_rows, rank = kept.shape

    def kernel(kept_ref, got_ref, own_ref, *away_refs):
        for d in range(places):
            own_ref[d] = kept_ref[d] + got_ref[d].astype(f32)
            for e, away_ref in enumerate(away_refs):
                k = (e + 1) * places + d
                away_ref[d] = (kept_ref[k] + got_ref[k].astype(f32)).astype(bf16)

    outs = [shape_of((places, half_rows, rank), f32)] + [shape_of((places, half_rows, rank), bf16)] * (lines - 1)
    return call(kernel, outs, [kept, got], [pltpu.VMEM] * 2, after=after)


def add_places(own, gots, places, after=()):
    _, half_rows, rank = own.shape

    def kernel(own_ref, *refs):
        got_refs, outs = refs[: len(gots)], refs[len(gots) :]
        for d in range(places):
            value = own_ref[d]
            for got_ref in got_refs:
                value = value + got_ref[d].astype(f32)
            outs[d][...] = value.astype(f32 if d == 0 else bf16)

    outs = [shape_of((half_rows, rank), f32)] + [shape_of((half_rows, rank), bf16)] * (places - 1)
    return call(kernel, outs, [own, *gots], [pltpu.VMEM] * (1 + len(gots)), after=after)


def down_gradient(at, shards, order, mine, theirs, t):
    count = len(shards)
    rows, depth = len(order) * t, shards[0].shape[1]
    half_rows, rank = mine.shape
    tile = tile_of(depth)

    def kernel(at_ref, mine_ref, theirs_ref, *refs):
        out_ref, back, placed, result, sems = refs[-5:]
        core, neur = at_ref[0], at_ref[1]
        back[pl.ds(pl.multiple_of(core * half_rows, half_rows), half_rows), :] = mine_ref[...].astype(f32)
        back[pl.ds(pl.multiple_of((1 - core) * half_rows, half_rows), half_rows), :] = theirs_ref[...].astype(f32)
        for i, s in enumerate(order):
            placed[i * t : (i + 1) * t, :] = back[pl.ds(pl.multiple_of((neur ^ s) * t, t), t), :]
        turned = placed[...].T.astype(bf16)
        copies = []
        for k in range(depth // tile):
            cols = slice(k * tile, (k + 1) * tile)
            whole = joined(refs[:count], cols)
            result[cols, :] = jnp.dot(turned, whole, preferred_element_type=f32).T
            copies.append(pltpu.make_async_copy(result.at[cols, :], out_ref.at[cols, :], sems.at[k]))
            copies[-1].start()
        for copy in copies:
            copy.wait()

    return call(
        kernel,
        [shape_of((depth, rank), f32)],
        [at, mine, theirs, *[held(shard) for shard in shards]],
        [pltpu.SMEM] + [pltpu.VMEM] * (2 + count),
        scratch=[
            pltpu.VMEM((rows, rank), f32),
            pltpu.VMEM((rows, rank), f32),
            pltpu.VMEM((depth, rank), f32),
            pltpu.SemaphoreType.DMA((depth // tile,)),
        ],
        out_spaces=[pl.ANY],
        mib=16,
    )[0]


def tuned_body(n_rows, n_neur, lines):
    places = n_neur // lines
    pairs_x = n_rows // 2

    def body(tokens, teacher_up, teacher_bias, predictor_down, predictor_up):
        row = lax.axis_index("rows")
        core = row % 2
        neur = lax.axis_index("neur")
        t = tokens.shape[0]
        half_rows = t * n_neur // 2
        width = teacher_up.shape[1] // n_rows
        rank = predictor_down.shape[1]
        row_at = jnp.reshape(row, (1,)).astype(jnp.int32)
        neur_at = jnp.reshape(neur, (1,)).astype(jnp.int32)
        mine_at = jnp.stack([core, neur]).astype(jnp.int32)
        other_at = jnp.stack([1 - core, neur]).astype(jnp.int32)

        def to_core(value):
            return flip(value, "rows", n_rows, 1)

        shards = {}

        orders = [
            [s for s in range(lines)],
            [s for s in range(lines, 2 * lines)],
            [d * lines for d in range(2, places)],
            [d * lines + e for e in range(1, lines) for d in range(2, places)],
        ]
        parts = {}
        away = list(range(1, pairs_x))
        splits = 1
        owns, arrived, got, mine_part, kept = {}, {}, {}, {}, {}
        (bias_cols,) = bias_part(row_at, teacher_bias, width, after=(neur_at, mine_at, other_at))
        gate = (bias_cols,)

        def blocks_of(chunk, distance, keep, cost=10**4, through=(), wait=False):
            nonlocal gate
            outs = partial_sums(
                row_at,
                parts[chunk],
                teacher_up,
                width,
                [(distance, keep, f32 if keep and distance == 0 else bf16)],
                gots=[got[chunk, distance]] if keep else None,
                pieces=[kept[distance, keep]] if chunk else None,
                retain=chunk == 0,
                split=splits,
                cost=cost,
                after=gate,
                through=through,
            )
            gate = (outs[0],)
            if keep:
                part, *outs = outs
                if distance == 0:
                    owns[chunk] = [part]
                elif wait:
                    outs.append(part)
                else:
                    arrived.setdefault(chunk, []).append(flip(part, "rows", n_rows, 2 * distance))
            else:
                got[chunk, distance] = [to_core(part) for part in outs[:splits]]
                outs = outs[splits:]
            if chunk == 0:
                kept[distance, keep], *outs = outs
            return outs

        def pin(*values, cost=10**4):
            nonlocal gate
            token, *values = hold(*values, after=gate, weight=cost)
            gate = (token,)
            return values

        def finish(chunks, before=None, through=(), beside=()):
            nonlocal gate
            relu, target, *passed = finish_preact(
                neur_at,
                bias_cols,
                [(orders[c], owns[c][0], arrived[c]) for c in chunks],
                t,
                n_neur,
                width,
                before,
                beside,
                after=gate,
                through=through,
            )
            gate = (target,)
            return (relu, target), passed

        def along_y(d):
            for e in range(1, lines):
                shards[d * lines + e] = flip(shards[d * lines], "neur", n_neur, e)

        BIG = 10**4
        shards = [tokens]
        shards += [flip(tokens, "neur", n_neur, e) for e in range(1, lines)]
        near = flip(tokens, "neur", n_neur, lines)
        far = [flip(tokens, "neur", n_neur, d * lines) for d in range(2, places)]
        parts[0] = shards
        for d in away:
            blocks_of(0, d, False, BIG)
        blocks_of(0, 0, False, BIG)
        (near,) = pin(near)
        parts[1] = [near] + [flip(near, "neur", n_neur, e) for e in range(1, lines)]
        for d in away:
            blocks_of(0, d, True, BIG)
        blocks_of(0, 0, True, BIG)
        for d in away:
            blocks_of(1, d, False)
        (far,) = stacked(far, True, after=gate)
        gate = (far,)
        parts[2] = [far]
        parts[3] = [flip(far, "neur", n_neur, e) for e in range(1, lines)]
        blocks_of(1, 0, False)
        for d in away:
            blocks_of(1, d, True)
        for d in away:
            blocks_of(2, d, False)
        done, _ = finish([0])
        blocks_of(1, 0, True)
        blocks_of(2, 0, False)
        for d in away:
            blocks_of(2, d, True)
        blocks_of(2, 0, True)
        pairs = [(rows_of[k], rows_of[k + 1]) for rows_of in orders for k in range(0, len(rows_of), 2)]
        hidden_keep, hidden_send = hidden_sums(
            row_at, [part for c in range(4) for part in parts[c]], predictor_down, orders, pairs, t, after=gate
        )
        gate = (hidden_keep,)
        hidden_got = to_core(hidden_send)
        done, _ = finish([1], done)
        for d in away:
            blocks_of(3, d, False)
        blocks_of(3, 0, False)
        (mine,) = add_all(f32, (hidden_keep, hidden_got), after=gate)
        gate = (mine,)
        moved = flip(mine, "rows", n_rows, 2)
        sends = [blocks_of(3, d, True, wait=True)[-1] for d in away]
        for d, part in zip(away, blocks_of(3, 0, True, through=sends)):
            arrived.setdefault(3, []).append(flip(part, "rows", n_rows, 2 * d))
        (moved,) = pin(moved)
        step = 4
        while step < n_rows:
            (mine,) = add_all(f32, (mine, moved))
            moved = flip(mine, "rows", n_rows, step)
            step *= 2
        (mine,) = add_all(bf16, (mine, moved), after=gate)
        gate = (mine,)
        column = [mine] + [flip(mine, "neur", n_neur, d * lines) for d in range(1, places)]
        own_lines = [flip(mine, "neur", n_neur, e) for e in range(1, lines)]
        done, _ = finish([2], done)
        (stack,) = stacked(column[1:], after=gate)
        gate = (stack,)
        stacks = [mine, stack]
        for e in range(1, lines):
            stacks += [own_lines[e - 1], flip(stack, "neur", n_neur, e)]
        others = [to_core(part) for part in stacks]
        (teacher_relu, target), _ = finish([3], done, beside=[predictor_up])
        (hidden,) = assemble_hidden(mine_at, [(pairs, stacks, others)], places, lines, t, rank, after=gate)

        half, send = residue_and_back(
            other_at, hidden, target, predictor_up, places, lines, half_rows, rank, bf16
        )
        residue, kept_back = residue_and_back(
            mine_at, hidden, target, predictor_up, places, lines, half_rows, rank, f32, half
        )
        back, *aways = add_lines(kept_back, to_core(send), places, lines)
        gots = [flip(value, "neur", n_neur, e + 1) for e, value in enumerate(aways)]
        grad_up = jnp.einsum("tr,tf->rf", hidden, residue, preferred_element_type=f32)
        back, *aways = add_places(back, gots, places, after=(grad_up,))
        gots = [flip(value, "neur", n_neur, (d + 1) * lines) for d, value in enumerate(aways)]
        (back,) = add_all(f32, (back, *gots))
        step = 2
        while step < n_rows:
            other = flip(back.astype(bf16), "rows", n_rows, step)
            back = back.astype(bf16).astype(f32) + other
            step *= 2
        back = back.astype(bf16)
        grad_down = down_gradient(
            mine_at, [part for c in range(4) for part in parts[c]], [s for c in orders for s in c], back, to_core(back), t
        )
        return (teacher_relu, grad_down, grad_up)

    return body


def solution(mesh):
    in_specs = (
        P("neur", "rows"),
        P("rows", "neur"),
        P("neur"),
        P("rows", "neur"),
        P(None, ("neur", "rows")),
    )
    out_specs = (P(None, ("neur", "rows")), P("rows", "neur"), P(None, ("neur", "rows")))
    n_rows, n_neur = mesh.shape["rows"], mesh.shape["neur"]
    lines = 1
    while lines * lines * 4 <= n_neur:
        lines *= 2
    tuned = tuned_body(n_rows, n_neur, lines)
    general = general_body(n_rows, n_neur)

    def body(tokens, teacher_up, teacher_bias, predictor_down, predictor_up):
        blocks = (teacher_up.shape[1] // n_rows, predictor_down.shape[1], predictor_up.shape[1])
        fits = all(size % 128 == 0 for size in blocks) and tokens.shape[0] % 16 == 0
        small = teacher_up.size * teacher_up.dtype.itemsize <= 40 * 2**20
        chosen = tuned if fits and small else general
        return chosen(tokens, teacher_up, teacher_bias, predictor_down, predictor_up)

    return jax.shard_map(body, mesh=mesh, in_specs=in_specs, out_specs=out_specs, check_vma=False)
```
